32 devices in a mesh: fsdp: 2 (over x), ctx: 4 (over z), tp: 4 (over y, core).
Axes of the slice: x: 2, y: 2, z: 4, core: 2. Of those that a mesh axis runs over, the one named last changes fastest.
Arguments:
- tokens: bfloat16 [4096, 768], P(('fsdp', 'ctx')), may hold values from -6 to 6
- g_attn: bfloat16 [768], P('fsdp'), may hold values from 0.5 to 1.5
- s_attn: bfloat16 [768], P('fsdp'), may hold values from -1.75 to 1.75
- w_query: bfloat16 [768, 768], P('fsdp', 'tp'), may hold values from -0.21875 to 0.21875
- b_query: bfloat16 [12, 64], P('tp', 'fsdp'), may hold values from -1.75 to 1.75
- w_key: bfloat16 [768, 768], P('fsdp', 'tp'), may hold values from -0.21875 to 0.21875
- w_value: bfloat16 [768, 768], P('fsdp', 'tp'), may hold values from -0.21875 to 0.21875
- b_value: bfloat16 [12, 64], P('tp', 'fsdp'), may hold values from -0.625 to 0.625
- w_out: bfloat16 [768, 768], P('tp', 'fsdp'), may hold values from -0.875 to 0.875
- b_out: bfloat16 [768], P('fsdp'), may hold values from -1.25 to 1.25
- g_mlp: bfloat16 [768], P('fsdp'), may hold values from 0.5 to 1.5
- s_mlp: bfloat16 [768], P('fsdp'), may hold values from -1.75 to 1.75
- w_up: bfloat16 [768, 3072], P('fsdp', 'tp'), may hold values from -0.21875 to 0.21875
- b_up: bfloat16 [12, 256], P('tp', 'fsdp'), may hold values from -1.75 to 1.75
- w_down: bfloat16 [3072, 768], P('tp', 'fsdp'), may hold values from -0.109375 to 0.109375
- b_down: bfloat16 [768], P('fsdp'), may hold values from -1.25 to 1.25
- cotangent: bfloat16 [4096, 768], P(('fsdp', 'ctx')), may hold values from -6 to 6
- lengths: int32 [2, 3], P('fsdp'), may hold values from 1 to 14, as said below
Outputs:
- layer_out: bfloat16 [4096, 768], P(('fsdp', 'ctx'))
- d_tokens: float32 [4096, 768], P(('fsdp', 'ctx'))
- dg_attn: float32 [768], P('fsdp')
- ds_attn: float32 [768], P('fsdp')
- dw_query: float32 [768, 768], P('fsdp', 'tp')
- db_query: float32 [12, 64], P('tp', 'fsdp')
- dw_key: float32 [768, 768], P('fsdp', 'tp')
- dw_value: float32 [768, 768], P('fsdp', 'tp')
- db_value: float32 [12, 64], P('tp', 'fsdp')
- dw_out: float32 [768, 768], P('tp', 'fsdp')
- db_out: float32 [768], P('fsdp')
- dg_mlp: float32 [768], P('fsdp')
- ds_mlp: float32 [768], P('fsdp')
- dw_up: float32 [768, 3072], P('fsdp', 'tp')
- db_up: float32 [12, 256], P('tp', 'fsdp')
- dw_down: float32 [3072, 768], P('tp', 'fsdp')
- db_down: float32 [768], P('fsdp')
The draws below stay inside these ranges and needn't reach their ends.
Inputs may be any that keep to these rules, and one draw needn't show every extreme that they name: `lengths`: each row sums to 16; in each row one sequence begins on a block of the first index of ctx and ends on a block of the last.
All inputs are finite; a program needn't handle non-finite values.
Results may differ from the reference program's by a relative error of at most 0.017.
Values may be sent and summed in bfloat16 or wider, within the bound.
No kernel may reach another device: no remote copies, remote signals or barrier semaphores. Data moves between devices by JAX's collectives and lax.ppermute only.
A program may use at most 128 MiB of HBM per device.

```python
import jax
import jax.numpy as jnp
from jax import lax

D = 768
H = 12
HD = 64
FF = 3072
BLK = 128
SEQS = 3
GROUPS = 2
GROUP = 2048
BLOCKS = 16
TOKENS = 4096


def draw_lengths(key, part):
    key = jax.random.fold_in(key, 11)
    key_one, key_two, key_place = jax.random.split(key, 3)
    groups = jnp.arange(GROUPS, dtype=jnp.int32)
    place = jax.random.randint(key_place, (GROUPS,), 0, SEQS, dtype=jnp.int32)
    raw_one = jax.random.randint(key_one, (GROUPS,), 1, 4, dtype=jnp.int32)
    raw_two = jax.random.randint(key_two, (GROUPS,), 1, 4, dtype=jnp.int32)
    edge = place != 1
    first_short = jnp.where(edge, jnp.minimum(raw_one, 2), raw_one)
    second_short = jnp.where(edge, jnp.minimum(raw_two, 3 - first_short), raw_two)
    first_short = jnp.where(groups == 0, 1, first_short)
    second_short = jnp.where(groups == 0, 1, second_short)
    longest = BLOCKS - first_short - second_short
    column_zero = jnp.where(place == 0, longest, first_short)
    column_one = jnp.where(place == 1, longest, jnp.where(place == 0, first_short, second_short))
    column_two = jnp.where(place == 2, longest, second_short)
    return jnp.stack([column_zero, column_one, column_two], axis=1).astype(jnp.int32)


def shard_levels(rng, shape, shards, low, top_value):
    level, own = 1.0, jax.random.fold_in(rng, 6)
    for position, shards_of in shards:
        draws = jnp.exp(jax.random.uniform(jax.random.fold_in(own, position), (shards_of,), jnp.float32, low / len(shards), top_value / len(shards)))
        level = level * jnp.repeat(draws, shape[position] // shards_of).reshape([-1 if axis == position else 1 for axis in range(len(shape))])
    return level


def gaussian(key, shape, scale, limit, cuts=(), kind=jnp.bfloat16):
    drawn = jax.random.normal(key, shape, jnp.float32) * scale
    if len(cuts) > 0:
        drawn = shard_levels(key, shape, cuts, -0.22, 0.18) * drawn
    return jnp.clip(drawn, min=-limit, max=limit).astype(kind)


def setup_inputs(seed: int = 0) -> dict:
    key_of = jax.random.split(jax.random.key(seed), 19)
    return {
        "tokens": gaussian(key_of[0], (TOKENS, D), 1.0, 6.0, ((0, 8),)),
        "g_attn": jnp.clip(1.0 + 0.1 * jax.random.normal(key_of[1], (D,), jnp.float32), 0.5, 1.5).astype(jnp.bfloat16),
        "s_attn": gaussian(key_of[2], (D,), 0.3, 1.75, ((0, 2),)),
        "w_query": gaussian(key_of[3], (D, D), D ** -0.5, 0.21875, ((0, 2), (1, 4))),
        "b_query": gaussian(key_of[4], (H, HD), 0.3, 1.75, ((0, 4), (1, 2))),
        "w_key": gaussian(key_of[5], (D, D), D ** -0.5, 0.21875, ((0, 2), (1, 4))),
        "w_value": gaussian(key_of[6], (D, D), D ** -0.5, 0.21875, ((0, 2), (1, 4))),
        "b_value": gaussian(key_of[7], (H, HD), 0.1, 0.625, ((0, 4), (1, 2))),
        "w_out": gaussian(key_of[8], (D, D), (D // 16) ** -0.5, 0.875, ((0, 4), (1, 2))),
        "b_out": gaussian(key_of[9], (D,), 0.2, 1.25, ((0, 2),)),
        "g_mlp": jnp.clip(1.0 + 0.1 * jax.random.normal(key_of[10], (D,), jnp.float32), 0.5, 1.5).astype(jnp.bfloat16),
        "s_mlp": gaussian(key_of[11], (D,), 0.3, 1.75, ((0, 2),)),
        "w_up": gaussian(key_of[12], (D, FF), D ** -0.5, 0.21875, ((0, 2), (1, 4))),
        "b_up": gaussian(key_of[13], (H, FF // H), 0.3, 1.75, ((0, 4), (1, 2))),
        "w_down": gaussian(key_of[14], (FF, D), FF ** -0.5, 0.109375, ((0, 4), (1, 2))),
        "b_down": gaussian(key_of[15], (D,), 0.2, 1.25, ((0, 2),)),
        "cotangent": gaussian(key_of[16], (TOKENS, D), 1.0, 6.0, ((0, 8),)),
        "lengths": draw_lengths(jax.random.fold_in(key_of[18], 71), 0),
    }


@jax.custom_vjp
def low(v):
    return lax.optimization_barrier(v.astype(jnp.bfloat16)).astype(jnp.float32)

@jax.custom_vjp
def low_back(v):
    return v

def low_keep(v):
    return (low(v), None)

def low_pass(kept, grad):
    return (grad,)

def back_keep(v):
    return (v, None)

def back_low(kept, grad):
    return (low(grad),)
low.defvjp(low_keep, low_pass)
low_back.defvjp(back_keep, back_low)
HIGH = lax.Precision.HIGHEST
EPS = 1e-05
NEG = -1e+30

def layer_norm(values, gain, shift):
    average = lax.optimization_barrier(jnp.mean(values, axis=-1, keepdims=True))
    centred = values - average
    spread = lax.optimization_barrier(jnp.mean(centred * centred, axis=-1, keepdims=True))
    return centred * lax.rsqrt(spread + EPS) * gain + shift

def smooth(values):
    return jax.nn.gelu(values, approximate=True)

def block_len(count):
    return 512 if count % 512 == 0 else count

def group_forward(weights, rows, documents):
    gain_one, shift_one, query_full, qbias_full, key_full, value_full, vbias_full, out_full, obias_full, gain_two, shift_two, up_full, ubias_full, down_full, dbias_full = weights
    count = rows.shape[0]
    normed_one = low(layer_norm(rows, gain_one, shift_one))
    queries = low(low_back(jnp.dot(normed_one, query_full, precision=HIGH) + qbias_full.reshape(-1)))
    queries = queries.reshape(count, H, HD)
    key_rows = low(low_back(jnp.dot(normed_one, key_full, precision=HIGH))).reshape(count, H, HD)
    values = low(low_back(jnp.dot(normed_one, value_full, precision=HIGH) + vbias_full.reshape(-1)))
    values = values.reshape(count, H, HD)
    places = jnp.arange(count, dtype=jnp.int32)
    query_len = block_len(count)

    def attend(index):
        start = index * query_len
        block = lax.dynamic_slice_in_dim(queries, start, query_len, 0)
        own_places = lax.dynamic_slice_in_dim(places, start, query_len, 0)
        own_docs = lax.dynamic_slice_in_dim(documents, start, query_len, 0)
        allowed = (places[None, :] <= own_places[:, None]) & (documents[None, :] == own_docs[:, None])
        raw = jnp.einsum('qhd,khd->hqk', block, key_rows, precision=HIGH) * HD ** (-0.5)
        scores = low_back(jnp.where(allowed[None], raw, NEG))
        peak = lax.optimization_barrier(jnp.max(scores, axis=-1, keepdims=True))
        expos = jnp.exp(scores - peak)
        probs = low(expos / lax.optimization_barrier(jnp.sum(expos, axis=-1, keepdims=True)))
        return jnp.einsum('hqk,khd->qhd', probs, values, precision=HIGH)
    mixed = lax.map(jax.checkpoint(attend), jnp.arange(count // query_len, dtype=jnp.int32))
    mixed = low(low_back(mixed.reshape(count, H * HD)))
    attention = low_back(jnp.dot(mixed, out_full, precision=HIGH) + obias_full)
    mid = rows + attention
    normed_two = low(layer_norm(mid, gain_two, shift_two))
    upper = low_back(jnp.dot(normed_two, up_full, precision=HIGH) + ubias_full.reshape(-1))
    active = low(smooth(upper))
    branch = low_back(jnp.dot(active, down_full, precision=HIGH) + dbias_full)
    return mid + branch

def reference(tokens, g_attn, s_attn, w_query, b_query, w_key, w_value, b_value, w_out, b_out, g_mlp, s_mlp, w_up, b_up, w_down, b_down, cotangent, lengths):
    weights = tuple((weight.astype(jnp.float32) for weight in (g_attn, s_attn, w_query, b_query, w_key, w_value, b_value, w_out, b_out, g_mlp, s_mlp, w_up, b_up, w_down, b_down)))
    rows = tokens.astype(jnp.float32)
    ends = (jnp.cumsum(lengths, axis=1) * BLK).astype(jnp.int32)
    places = jnp.arange(GROUP, dtype=jnp.int32)
    documents = lax.optimization_barrier(jnp.sum((places[None, :, None] >= ends[:, None, :]).astype(jnp.int32), axis=2, dtype=jnp.int32))

    def forward(weights, rows):

        def step(carry, item):
            return (carry, jax.checkpoint(group_forward)(weights, item[0], item[1]))
        _, outputs = lax.scan(step, jnp.zeros((), jnp.float32), (rows.reshape(GROUPS, GROUP, D), documents))
        return outputs.reshape(TOKENS, D)
    result, backward = jax.vjp(forward, weights, rows)
    grad_weights, grad_rows = backward(cotangent.astype(jnp.float32))
    return (result.astype(jnp.bfloat16), grad_rows, grad_weights[0], grad_weights[1], grad_weights[2], grad_weights[3], grad_weights[4], grad_weights[5], grad_weights[6], grad_weights[7], grad_weights[8], grad_weights[9], grad_weights[10], grad_weights[11], grad_weights[12], grad_weights[13], grad_weights[14])
```

```python
import functools

import jax
import jax.numpy as jnp
from jax import lax
from jax.experimental import pallas as pl
from jax.experimental.pallas import tpu as pltpu
from jax.sharding import PartitionSpec as P

HD = 64
BLK = 128
EPS = 1e-05
NEG = -1e30
F32 = jnp.float32
BF16 = jnp.bfloat16
CTX, FSDP, TP, ENDS = 0, 1, 2, 3
GELU_C = 0.7978845608028654
GELU_A = 0.044715


def shape(dims, kind):
    return jax.ShapeDtypeStruct(dims, kind)


def call(body, outs, scal, *args, scratch=(), name=None):
    vmem = pl.BlockSpec(memory_space=pltpu.VMEM)
    return pl.pallas_call(
        body,
        out_shape=outs,
        in_specs=[pl.BlockSpec(memory_space=pltpu.SMEM)] + [vmem] * len(args),
        out_specs=[vmem] * len(outs),
        scratch_shapes=list(scratch),
        compiler_params=pltpu.CompilerParams(vmem_limit_bytes=48 * 1024 * 1024),
        name=name,
    )(scal, *args)


def nn(a, b):
    return jnp.dot(a, b, preferred_element_type=F32)


def nt(a, b):
    return lax.dot_general(a, b, (((1,), (1,)), ((), ())), preferred_element_type=F32)


def standard(rows):
    average = jnp.mean(rows, axis=-1, keepdims=True)
    centred = rows - average
    spread = jnp.mean(centred * centred, axis=-1, keepdims=True)
    scale = lax.rsqrt(spread + EPS)
    return centred * scale, scale


def norm_back(xhat, scale, gain, grad):
    e = grad * gain
    return scale * (
        e
        - jnp.mean(e, axis=-1, keepdims=True)
        - xhat * jnp.mean(e * xhat, axis=-1, keepdims=True)
    )


def place(ref, parts, index, axis):
    if len(parts) == 1:
        ref[...] = parts[0][...]
        return
    size = parts[0].shape[axis]
    for part, slot in zip(parts, (index, 1 - index)):
        span = pl.ds(pl.multiple_of(slot * size, size), size)
        if axis == 0:
            ref[span, :] = part[...]
        else:
            ref[:, span] = part[...]


def mask_bias(scal, seqs, query_block, key_block, size, diagonal):
    places = lax.broadcasted_iota(jnp.int32, (1, size), 1) + query_block * size
    first = jnp.zeros((1, size), jnp.int32)
    for i in range(seqs):
        end = scal[ENDS + i]
        first = jnp.where(places >= end, end, first)
    keys = lax.broadcasted_iota(jnp.int32, (size, size), 0) + key_block * size
    seen = keys >= first
    if diagonal:
        seen = seen & (keys <= places)
    return jnp.where(seen, 0.0, NEG)


def attend(heads, q, kv, bias, state, acc):
    width = heads * HD
    values_t = kv[:, width:].T
    for h in range(heads):
        cut = slice(h * HD, (h + 1) * HD)
        scores = nt(kv[:, cut], q[:, cut]) + bias
        peak = state[h : h + 1, :]
        total = state[heads + h : heads + h + 1, :]
        new_peak = jnp.maximum(peak, jnp.max(scores, axis=0, keepdims=True))
        fade = jnp.exp(peak - new_peak)
        probs = jnp.exp(scores - new_peak)
        state[h : h + 1, :] = new_peak
        state[heads + h : heads + h + 1, :] = total * fade + jnp.sum(probs, axis=0, keepdims=True)
        acc[cut, :] = acc[cut, :] * fade + nn(values_t[cut, :], probs.astype(BF16))


def first_kernel(heads, seqs, count, scal, tokens, vecs, *refs):
    parts, (full, normed, q_out, qt_out, kv_out, state, acc) = refs[:count], refs[count:]
    width = heads * HD
    size = tokens.shape[0]
    place(full, parts, scal[FSDP], 0)
    xhat, _ = standard(tokens[...].astype(F32))
    low = (xhat * vecs[0:1, :] + vecs[1:2, :]).astype(BF16)
    normed[...] = low
    rows = nn(low, full[...])
    bias = jnp.concatenate(
        [jnp.zeros((1, width), F32), vecs[8:9, :width], vecs[7:8, :width]], axis=1
    )
    rows = (rows + bias).astype(BF16)
    q = rows[:, 2 * width :] * jnp.asarray(HD**-0.5, BF16)
    kv = rows[:, : 2 * width]
    q_out[...] = q
    qt_out[...] = q.T
    kv_out[...] = kv
    state[...] = jnp.where(
        lax.broadcasted_iota(jnp.int32, state.shape, 0) < heads, jnp.float32(NEG), 0.0
    )
    acc[...] = jnp.zeros_like(acc)
    mask = mask_bias(scal, seqs, scal[CTX], scal[CTX], size, True)
    attend(heads, q, kv, mask, state, acc)


def step_kernel(heads, seqs, count, step, last, scal, vecs, full, q, state_in, acc_in, *refs):
    parts, refs = refs[:count], refs[count:]
    if last:
        kv_out, mixed_t, mix_t, logs, state, acc, tokens = refs
    else:
        kv_out, state, acc, tokens = refs
    width = heads * HD
    size = q.shape[0]
    state[...] = state_in[...]
    acc[...] = acc_in[...]

    @pl.when(scal[CTX] >= step)
    def _():
        place(tokens, parts, lax.rem(scal[TP], 2), 0)
        xhat, _ = standard(tokens[...].astype(F32))
        low = (xhat * vecs[0:1, :] + vecs[1:2, :]).astype(BF16)
        rows = nn(low, full[:, : 2 * width])
        bias = jnp.concatenate([jnp.zeros((1, width), F32), vecs[8:9, :width]], axis=1)
        kv = (rows + bias).astype(BF16)
        kv_out[...] = kv
        mask = mask_bias(scal, seqs, scal[CTX], scal[CTX] - step, size, False)
        attend(heads, q[...], kv, mask, state, acc)

    @pl.when(scal[CTX] < step)
    def _():
        kv_out[...] = jnp.zeros_like(kv_out)

    if last:
        logs[...] = jnp.zeros_like(logs)
        for h in range(heads):
            cut = slice(h * HD, (h + 1) * HD)
            total = state[heads + h : heads + h + 1, :]
            mix = acc[cut, :] / total
            mix_t[cut, :] = mix
            mixed_t[cut, :] = mix.astype(BF16)
            logs[h : h + 1, :] = state[h : h + 1, :] + jnp.log(total)


def mlp_kernel(count, scal, tokens, cotangent, vecs, *refs):
    mixed, refs = refs[:4], refs[4:]
    out_parts, refs = refs[:4], refs[4:]
    up_parts, refs = refs[:count], refs[count:]
    down_parts, refs = refs[:count], refs[count:]
    (mid_out, two_out, active_out, grad_out, terms_out, keep, send1, send2, send3) = refs[:9]
    up, down, back = refs[9:]
    index = scal[FSDP]
    place(up, up_parts, index, 0)
    place(down, down_parts, index, 1)
    mid = tokens[...].astype(F32) + vecs[2:3, :]
    total = nn(mixed[0][...].T, out_parts[0][...])
    for i in range(1, 4):
        total += nn(mixed[i][...].T, out_parts[i][...])
    mid = mid + total
    mid_out[...] = mid
    xhat, _ = standard(mid)
    two = (xhat * vecs[3:4, :] + vecs[4:5, :]).astype(BF16)
    two_out[...] = two
    v = nn(two, up[...]) + vecs[6:7, :]
    t = jnp.tanh(GELU_C * (v + GELU_A * (v * v * v)))
    active = (0.5 * v * (1.0 + t)).astype(BF16)
    active_out[...] = active
    slope = 0.5 * (1.0 + t) + 0.5 * v * (1.0 - t * t) * (GELU_C * (1.0 + 3.0 * GELU_A * (v * v)))
    grad = (nt(cotangent[...], down[...]) * slope).astype(BF16)
    grad_out[...] = grad
    back[...] = nt(grad, up[...])
    size = keep.shape[0]
    for i, out in enumerate((keep, send1, send2, send3)):
        slot = jnp.bitwise_xor(scal[TP], i)
        out[...] = back[pl.ds(pl.multiple_of(slot * size, size), size), :].astype(out.dtype)
    terms_out[...] = nn(active, down[...]).astype(BF16)


def mid_back_kernel(scal, mid, cotangent, vecs, keep, got1, got2, got3, mid_grad, attn_grad, sums):
    size = keep.shape[0]
    rows = pl.ds(pl.multiple_of(scal[TP] * size, size), size)
    grad = keep[...] + got1[...].astype(F32) + got2[...].astype(F32) + got3[...].astype(F32)
    xhat, scale = standard(mid[rows, :])
    total = cotangent[rows, :].astype(F32) + norm_back(xhat, scale, vecs[3:4, :], grad)
    mid_grad[...] = total
    attn_grad[...] = total.astype(BF16)
    sums[...] = jnp.zeros_like(sums)
    sums[0:1, :] = jnp.sum(grad * xhat, axis=0, keepdims=True)
    sums[1:2, :] = jnp.sum(grad, axis=0, keepdims=True)


def pieces_of(value):
    one = value.astype(BF16).astype(F32)
    two = (value - one).astype(BF16).astype(F32)
    return one, two, value - one - two


def out_back_kernel(heads, scal, w_out, mix_t, logs, part0, part1, part2, part3, rows, pack):
    width = heads * HD
    size = part0.shape[0]
    for i, part in enumerate((part0, part1, part2, part3)):
        slot = jnp.bitwise_xor(scal[TP], i)
        rows[pl.ds(pl.multiple_of(slot * size, size), size), :] = part[...]
    grad_t = nt(w_out[...], rows[...]).astype(BF16)
    pack[:width, :] = grad_t
    wide = grad_t.astype(F32) * mix_t[...]
    stats = [logs[h : h + 1, :] for h in range(heads)]
    stats += [
        jnp.sum(wide[h * HD : (h + 1) * HD, :], axis=0, keepdims=True) for h in range(heads)
    ]
    lines = []
    for stat in stats:
        lines += list(pieces_of(stat))
    lines.append(jnp.zeros((32 - len(lines), rows.shape[0]), F32))
    pack[width:, :] = jnp.concatenate(lines, axis=0).astype(BF16)


def read_stats(heads, pack):
    lines = pack[heads * HD :, :].astype(F32)
    stats = [
        lines[3 * i : 3 * i + 1, :] + lines[3 * i + 1 : 3 * i + 2, :] + lines[3 * i + 2 : 3 * i + 3, :]
        for i in range(2 * heads)
    ]
    return stats[:heads], stats[heads:]


def pair_back(heads, h, q, grad, kv, bias, logs, deltas):
    width = heads * HD
    cut = slice(h * HD, (h + 1) * HD)
    cut_v = slice(width + h * HD, width + (h + 1) * HD)
    probs = jnp.exp(nt(kv[:, cut], q[:, cut]) + bias - logs[h])
    grad_probs = nt(kv[:, cut_v], grad[:, cut])
    return probs.astype(BF16), (probs * (grad_probs - deltas[h])).astype(BF16)


def query_kernel(heads, seqs, count, scal, q, pack, *refs):
    kvs, (dq_out, acc, dq_t) = refs[:count], refs[count:]
    width = heads * HD
    size = q.shape[0]
    logs, deltas = read_stats(heads, pack)
    grad = pack[:width, :].T
    for step in range(count):

        def work(step=step):
            kv = kvs[step][...]
            keys_t = kv[:, :width].T
            bias = mask_bias(scal, seqs, scal[CTX], scal[CTX] - step, size, step == 0)
            for h in range(heads):
                cut = slice(h * HD, (h + 1) * HD)
                cut_v = slice(width + h * HD, width + (h + 1) * HD)
                probs, grads = pair_back(heads, h, q[...], grad, kv, bias, logs, deltas)
                term = nn(keys_t[cut, :], grads)
                if step == 0:
                    dq_t[cut, :] = term
                    acc[:, cut] = nn(grads, q[:, cut])
                    acc[:, cut_v] = nn(probs, grad[:, cut])
                else:
                    dq_t[cut, :] += term

        if step == 0:
            work()
        else:
            pl.when(scal[CTX] >= step)(work)
    dq_out[...] = (dq_t[...] * (HD**-0.5)).T.astype(BF16)


def key_kernel(heads, seqs, step, blocks, last, scal, kv, q_t, pack, acc_in, acc):
    width = heads * HD
    size = kv.shape[0]
    if last:
        acc[...] = acc_in[...].astype(acc.dtype)
    else:
        acc[...] = acc_in[...]

    @pl.when(scal[CTX] + step < blocks)
    def _():
        logs, deltas = read_stats(heads, pack)
        grad = pack[:width, :].T
        q = q_t[...].T
        bias = mask_bias(scal, seqs, scal[CTX] + step, scal[CTX], size, False)
        for h in range(heads):
            cut = slice(h * HD, (h + 1) * HD)
            cut_v = slice(width + h * HD, width + (h + 1) * HD)
            probs, grads = pair_back(heads, h, q, grad, kv[...], bias, logs, deltas)
            acc[:, cut] = (acc_in[:, cut] + nn(grads, q[:, cut])).astype(acc.dtype)
            acc[:, cut_v] = (acc_in[:, cut_v] + nn(probs, grad[:, cut])).astype(acc.dtype)


def split_store(scal, lead, value, outs):
    if len(outs) == 1:
        outs[0][lead] = value
        return
    mine, theirs, hold = outs
    size = mine.shape[1]
    hold[...] = value
    index = scal[FSDP]
    mine[lead] = hold[pl.ds(pl.multiple_of(index * size, size), size), :]
    theirs[lead] = hold[pl.ds(pl.multiple_of((1 - index) * size, size), size), :].astype(BF16)


def mlp_grads_kernel(scal, two, grad, active, cotangent, sums, *outs):
    split_store(scal, 0, nn(two[...].T, grad[...]), outs)
    split_store(scal, 1, nn(cotangent[...].T, active[...]), outs)
    sums[...] = jnp.zeros_like(sums)
    sums[0:1, :] = jnp.sum(grad[...].astype(F32), axis=0, keepdims=True)
    sums[1:2, :] = jnp.sum(cotangent[...].astype(F32), axis=0, keepdims=True)


def query_grads_kernel(scal, normed, dq, attn_grad, mixed_t, sums, *outs):
    left = nn(normed[...].T, dq[...])
    right = nt(attn_grad[...].T, mixed_t[...])
    split_store(scal, 0, jnp.concatenate([left, right], axis=1), outs)
    width = dq.shape[1]
    sums[...] = jnp.zeros_like(sums)
    sums[0:1, :] = jnp.sum(attn_grad[...].astype(F32), axis=0, keepdims=True)
    sums[1:2, :width] = jnp.sum(dq[...].astype(F32), axis=0, keepdims=True)


def key_grads_kernel(scal, normed, dkv, sums, *outs):
    split_store(scal, 0, nn(normed[...].T, dkv[...]), outs)
    width = dkv.shape[1] // 2
    sums[...] = jnp.zeros_like(sums)
    sums[0:1, : 2 * width] = jnp.sum(dkv[...].astype(F32), axis=0, keepdims=True)


def head_back_kernel(scal, full, dq, dkv, keep, send1, send2, send3, back):
    width = dq.shape[1]
    back[...] = nt(dkv[...], full[:, : 2 * width]) + nt(dq[...], full[:, 2 * width :])
    size = keep.shape[0]
    for i, out in enumerate((keep, send1, send2, send3)):
        slot = jnp.bitwise_xor(scal[TP], i)
        out[...] = back[pl.ds(pl.multiple_of(slot * size, size), size), :].astype(out.dtype)


def one_back_kernel(scal, tokens, vecs, mid_grad, keep, got1, got2, got3, out, sums):
    size = keep.shape[0]
    rows = pl.ds(pl.multiple_of(scal[TP] * size, size), size)
    grad = keep[...] + got1[...].astype(F32) + got2[...].astype(F32) + got3[...].astype(F32)
    xhat, scale = standard(tokens[rows, :].astype(F32))
    total = mid_grad[...] + norm_back(xhat, scale, vecs[0:1, :], grad)
    out[...] = total.astype(BF16)
    sums[...] = jnp.zeros_like(sums)
    sums[0:1, :] = jnp.sum(grad * xhat, axis=0, keepdims=True)
    sums[1:2, :] = jnp.sum(grad, axis=0, keepdims=True)


def join_kernel(scal, part0, part1, part2, part3, out):
    size = part0.shape[0]
    for i, part in enumerate((part0, part1, part2, part3)):
        slot = jnp.bitwise_xor(scal[TP], i)
        out[pl.ds(pl.multiple_of(slot * size, size), size), :] = part[...].astype(out.dtype)


def swap_fsdp(value):
    return lax.ppermute(value, "fsdp", [(0, 1), (1, 0)])


def swap_tp(value, bits):
    return lax.ppermute(value, "tp", [(i, i ^ bits) for i in range(4)])


def gather_tp(value):
    far = swap_tp(value, 2)
    near = swap_tp(value, 1)
    return value, near, far, swap_tp(far, 1)


def up_ctx(value, step):
    count = lax.axis_size("ctx")
    return lax.ppermute(value, "ctx", [(i, i + step) for i in range(count - step)])


def down_ctx(value, step):
    count = lax.axis_size("ctx")
    return lax.ppermute(value, "ctx", [(i + step, i) for i in range(count - step)])


def chain_ctx(value, inner):
    part = value.astype(BF16)
    got = lax.ppermute(part, "ctx", [(0, 1), (3, 2)])
    part = (value + got.astype(F32)).astype(BF16)
    got = lax.ppermute(part, "ctx", [(1, 2), (2, 1)])
    part = (part.astype(F32) + got.astype(F32)).astype(BF16)
    got = lax.ppermute(part, "ctx", [(1, 0), (2, 3)])
    return jnp.where(inner, part, got)


def shards(
    tokens,
    g_attn,
    s_attn,
    w_query,
    b_query,
    w_key,
    w_value,
    b_value,
    w_out,
    b_out,
    g_mlp,
    s_mlp,
    w_up,
    b_up,
    w_down,
    b_down,
    cotangent,
    lengths,
):
    owners = lax.axis_size("fsdp")
    blocks = lax.axis_size("ctx")
    pair = owners == 2
    count = 2 if pair else 1
    size, model = tokens.shape
    heads = b_query.shape[0]
    width = heads * HD
    hidden = w_up.shape[1]
    seqs = lengths.shape[1]
    quarter = size // 4
    ctx = lax.axis_index("ctx")
    fsdp = lax.axis_index("fsdp")
    tp = lax.axis_index("tp")
    inner = (ctx == 1) | (ctx == 2)
    ends = jnp.cumsum(lengths[0]) * BLK
    scal = jnp.concatenate([jnp.stack([ctx, fsdp, tp]).astype(jnp.int32), ends.astype(jnp.int32)])

    def fetch(value, axis):
        if pair:
            return (value, swap_fsdp(value))
        return (lax.all_gather(value, "fsdp", axis=axis, tiled=True),)

    w_qkv = fetch(jnp.concatenate([w_key, w_value, w_query], axis=1), 0)
    share = model // owners
    flat = jnp.concatenate(
        [
            g_attn,
            s_attn,
            b_out,
            g_mlp,
            s_mlp,
            b_down,
            b_up.reshape(-1),
            b_query.reshape(-1),
            b_value.reshape(-1),
        ]
    )
    if pair:
        flat_other = swap_fsdp(flat)
        flats = jnp.stack(
            [jnp.where(fsdp == 0, flat, flat_other), jnp.where(fsdp == 0, flat_other, flat)]
        )
    else:
        flats = lax.all_gather(flat, "fsdp", axis=0)
    flats = flats.astype(F32)
    singles = flats[:, : 6 * share].reshape(owners, 6, share).transpose(1, 0, 2).reshape(6, model)
    at = 6 * share

    def rows_of(start, total):
        cut = flats[:, start : start + total // owners].reshape(owners, heads, -1)
        return jnp.pad(cut.transpose(1, 0, 2).reshape(1, total), ((0, 0), (0, model - total)))

    vecs = jnp.concatenate(
        [
            singles,
            rows_of(at, hidden),
            rows_of(at + hidden // owners, width),
            rows_of(at + (hidden + width) // owners, width),
            jnp.zeros((7, model), F32),
        ]
    )
    half = lax.dynamic_slice_in_dim(tokens, (tp % 2) * (size // 2), size // 2, 0)
    lower = []
    for step in range(1, blocks):
        got = up_ctx(half, step)
        lower.append((got, swap_tp(got, 1)))
    out_own = fetch(w_out, 1)
    up_parts = fetch(w_up, 0)
    down_parts = fetch(w_down, 1)
    if pair:
        out_full = jnp.where(
            fsdp == 0,
            jnp.concatenate(out_own, axis=1),
            jnp.concatenate(out_own[::-1], axis=1),
        )
    else:
        out_full = out_own[0]
    out_parts = gather_tp(out_full)

    state_shape = shape((8, size), F32)
    acc_shape = shape((width, size), F32)
    full, normed, q, q_t, kv, state, acc = call(
        functools.partial(first_kernel, heads, seqs, count),
        [
            shape((model, 3 * width), BF16),
            shape((size, model), BF16),
            shape((size, width), BF16),
            shape((width, size), BF16),
            shape((size, 2 * width), BF16),
            state_shape,
            acc_shape,
        ],
        scal,
        tokens,
        vecs,
        *w_qkv,
        name="attend_first",
    )
    upper_q = [down_ctx(q_t, step) for step in range(1, blocks)]
    kvs = [kv]
    for step in range(1, blocks):
        last = step == blocks - 1
        outs = [shape((size, 2 * width), BF16)]
        scratch = [pltpu.VMEM((size, model), BF16)]
        if last:
            outs += [shape((width, size), BF16), acc_shape, state_shape]
            scratch = [pltpu.VMEM((8, size), F32), pltpu.VMEM((width, size), F32)] + scratch
        else:
            outs += [state_shape, acc_shape]
        got = call(
            functools.partial(step_kernel, heads, seqs, 2, step, last),
            outs,
            scal,
            vecs,
            full,
            q,
            state,
            acc,
            *lower[step - 1],
            scratch=scratch,
            name="attend_step",
        )
        kvs.append(got[0])
        if last:
            mixed_t, mix_t, logs = got[1:]
        else:
            state, acc = got[1:]

    mixed_parts = gather_tp(mixed_t)
    row_quarter = shape((quarter, model), BF16)
    wide = shape((size, hidden), BF16)
    mid, two, active, grad_upper, terms, *back = call(
        functools.partial(mlp_kernel, count),
        [
            shape((size, model), F32),
            shape((size, model), BF16),
            wide,
            wide,
            shape((size, model), BF16),
            shape((quarter, model), F32),
            row_quarter,
            row_quarter,
            row_quarter,
        ],
        scal,
        tokens,
        cotangent,
        vecs,
        *mixed_parts,
        *out_parts,
        *up_parts,
        *down_parts,
        scratch=[
            pltpu.VMEM((model, hidden), BF16),
            pltpu.VMEM((hidden, model), BF16),
            pltpu.VMEM((size, model), F32),
        ],
        name="mlp",
    )
    got = [swap_tp(back[i], i) for i in range(1, 4)]
    layer_out = (
        mid + lax.psum(terms, "tp").astype(F32) + vecs[5:6, :]
    ).astype(BF16)

    def grad_outs(lead, columns):
        if pair:
            dims = (lead, share, columns)
            return [shape(dims, F32), shape(dims, BF16)], [pltpu.VMEM((model, columns), F32)]
        return [shape((lead, model, columns), F32)], []

    def owned(parts):
        if pair:
            return parts[0] + swap_fsdp(parts[1]).astype(F32)
        return lax.psum_scatter(parts[0], "fsdp", scatter_dimension=1, tiled=True)

    sums_shape = shape((8, model), F32)
    mid_grad, attn_quarter, sums_mid = call(
        mid_back_kernel,
        [shape((quarter, model), F32), row_quarter, sums_shape],
        scal,
        mid,
        cotangent,
        vecs,
        back[0],
        *got,
        name="mid_back",
    )
    attn_parts = gather_tp(attn_quarter)
    outs, scratch = grad_outs(2, hidden)
    sums_mlp, *parts_mlp = call(
        mlp_grads_kernel,
        [sums_shape] + outs,
        scal,
        two,
        grad_upper,
        active,
        cotangent,
        scratch=scratch,
        name="mlp_grads",
    )
    attn_grad, pack = call(
        functools.partial(out_back_kernel, heads),
        [shape((size, model), BF16), shape((width + 32, size), BF16)],
        scal,
        out_full,
        mix_t,
        logs,
        *attn_parts,
        name="out_back",
    )
    upper_pack = [down_ctx(pack, step) for step in range(1, blocks)]
    dq, dkv = call(
        functools.partial(query_kernel, heads, seqs, blocks),
        [shape((size, width), BF16), shape((size, 2 * width), F32)],
        scal,
        q,
        pack,
        *kvs,
        scratch=[pltpu.VMEM((width, size), F32)],
        name="query_back",
    )
    outs, scratch = grad_outs(1, 2 * width)
    sums_query, *parts_query = call(
        query_grads_kernel,
        [sums_shape] + outs,
        scal,
        normed,
        dq,
        attn_grad,
        mixed_t,
        scratch=scratch,
        name="query_grads",
    )
    for step in range(1, blocks):
        last = step == blocks - 1
        (dkv,) = call(
            functools.partial(key_kernel, heads, seqs, step, blocks, last),
            [shape((size, 2 * width), BF16 if last else F32)],
            scal,
            kv,
            upper_q[step - 1],
            upper_pack[step - 1],
            dkv,
            name="key_back",
        )
    *back, = call(
        head_back_kernel,
        [shape((quarter, model), F32), row_quarter, row_quarter, row_quarter],
        scal,
        full,
        dq,
        dkv,
        scratch=[pltpu.VMEM((size, model), F32)],
        name="head_back",
    )
    got = [swap_tp(back[i], i) for i in range(1, 4)]
    outs, scratch = grad_outs(1, 2 * width)
    sums_key, *parts_key = call(
        key_grads_kernel,
        [sums_shape] + outs,
        scal,
        normed,
        dkv,
        scratch=scratch,
        name="key_grads",
    )
    token_quarter, sums_one = call(
        one_back_kernel,
        [row_quarter, sums_shape],
        scal,
        tokens,
        vecs,
        mid_grad,
        back[0],
        *got,
        name="one_back",
    )
    (d_tokens,) = call(
        join_kernel, [shape((size, model), F32)], scal, *gather_tp(token_quarter), name="join"
    )

    total_mlp = chain_ctx(owned(parts_mlp), inner).astype(F32)
    total_query = chain_ctx(owned(parts_query), inner).astype(F32)[0]
    total_key = chain_ctx(owned(parts_key), inner).astype(F32)[0]
    first = (tp == 0).astype(F32)
    own_rows = jnp.concatenate(
        [
            sums_mlp[0:1],
            jnp.pad(sums_query[1:2, :width], ((0, 0), (0, model - width))),
            jnp.pad(sums_key[0:1, width : 2 * width], ((0, 0), (0, model - width))),
            jnp.zeros((1, model), F32),
        ]
    )
    slots = (jnp.arange(4)[:, None, None] == tp).astype(F32) * own_rows[None]
    small = jnp.concatenate(
        [
            sums_one[0:2],
            sums_mid[0:2],
            sums_query[0:1] * first,
            sums_mlp[1:2] * first,
            jnp.zeros((2, model), F32),
            slots.reshape(16, model),
        ]
    )
    small = lax.psum(small, ("fsdp", "ctx", "tp"))
    shared = lax.dynamic_slice_in_dim(small[:6], fsdp * share, share, 1)
    own = lax.dynamic_slice_in_dim(small[8:], tp * 4, 4, 0)

    def by_head(row, total):
        cut = row[:total].reshape(heads, total // heads)
        return lax.dynamic_slice_in_dim(cut, fsdp * (total // heads // owners), total // heads // owners, 1)

    return (
        layer_out,
        d_tokens,
        shared[0],
        shared[1],
        total_query[:, :width],
        by_head(own[1], width),
        total_key[:, :width],
        total_key[:, width:],
        by_head(own[2], width),
        total_query[:, width:].T,
        shared[4],
        shared[2],
        shared[3],
        total_mlp[0],
        by_head(own[0], hidden),
        total_mlp[1].T,
        shared[5],
    )


def solution(mesh):
    return jax.shard_map(
        shards,
        mesh=mesh,
        in_specs=(
            P(("fsdp", "ctx"), None),
            P("fsdp"),
            P("fsdp"),
            P("fsdp", "tp"),
            P("tp", "fsdp"),
            P("fsdp", "tp"),
            P("fsdp", "tp"),
            P("tp", "fsdp"),
            P("tp", "fsdp"),
            P("fsdp"),
            P("fsdp"),
            P("fsdp"),
            P("fsdp", "tp"),
            P("tp", "fsdp"),
            P("tp", "fsdp"),
            P("fsdp"),
            P(("fsdp", "ctx"), None),
            P("fsdp", None),
        ),
        out_specs=(
            P(("fsdp", "ctx"), None),
            P(("fsdp", "ctx"), None),
            P("fsdp"),
            P("fsdp"),
            P("fsdp", "tp"),
            P("tp", "fsdp"),
            P("fsdp", "tp"),
            P("fsdp", "tp"),
            P("tp", "fsdp"),
            P("tp", "fsdp"),
            P("fsdp"),
            P("fsdp"),
            P("fsdp"),
            P("fsdp", "tp"),
            P("tp", "fsdp"),
            P("tp", "fsdp"),
            P("fsdp"),
        ),
        check_vma=False,
    )
```

```python
import functools

import jax
import jax.numpy as jnp
from jax import lax
from jax.experimental import pallas as pl
from jax.experimental.pallas import tpu as pltpu
from jax.sharding import PartitionSpec as P

HD = 64
BLK = 128
EPS = 1e-05
NEG = -1e30
F32 = jnp.float32
BF16 = jnp.bfloat16
CTX, FSDP, TP, LENGTHS = 0, 1, 2, 3
GELU_C = 0.7978845608028654
GELU_A = 0.044715


def shape(dims, kind):
    return jax.ShapeDtypeStruct(dims, kind)


def call(body, outs, scal, *args, cost=1.0, scratch=(), name=None, staged=False):
    def spec(value):
        if staged:
            return pl.BlockSpec(memory_space=pltpu.VMEM)
        return pl.BlockSpec(value.shape, lambda i: (0,) * len(value.shape))

    return pl.pallas_call(
        body,
        grid=() if staged else (1,),
        out_shape=outs,
        in_specs=[pl.BlockSpec(memory_space=pltpu.SMEM)] + [spec(arg) for arg in args],
        out_specs=[spec(out) for out in outs],
        scratch_shapes=list(scratch),
        compiler_params=pltpu.CompilerParams(vmem_limit_bytes=62 * 1024 * 1024),
        cost_estimate=pl.CostEstimate(
            flops=int(cost * 4e9), bytes_accessed=int(cost * 12e6), transcendentals=0
        ),
        name=name,
    )(scal, *args)


def after(value, *others):
    return lax.optimization_barrier((value,) + others)[0]


def nn(a, b):
    return jnp.dot(a, b, preferred_element_type=F32)


def nt(a, b):
    return lax.dot_general(a, b, (((1,), (1,)), ((), ())), preferred_element_type=F32)


def standard(rows):
    average = jnp.mean(rows, axis=-1, keepdims=True)
    centred = rows - average
    spread = jnp.mean(centred * centred, axis=-1, keepdims=True)
    scale = lax.rsqrt(spread + EPS)
    return centred * scale, scale


def norm_back(xhat, scale, gain, grad):
    e = grad * gain
    return scale * (
        e
        - jnp.mean(e, axis=-1, keepdims=True)
        - xhat * jnp.mean(e * xhat, axis=-1, keepdims=True)
    )


def place(ref, parts, index, axis):
    if len(parts) == 1:
        ref[...] = parts[0][...]
        return
    size = parts[0].shape[axis]
    for part, slot in zip(parts, (index, 1 - index)):
        span = pl.ds(pl.multiple_of(slot * size, size), size)
        if axis == 0:
            ref[span, :] = part[...]
        else:
            ref[:, span] = part[...]


def mask_bias(scal, seqs, query_block, key_block, size, diagonal):
    places = lax.broadcasted_iota(jnp.int32, (1, size), 1) + query_block * size
    first = jnp.zeros((1, size), jnp.int32)
    end = 0
    for i in range(seqs):
        end = end + scal[LENGTHS + i] * BLK
        first = jnp.where(places >= end, end, first)
    keys = lax.broadcasted_iota(jnp.int32, (size, size), 0) + key_block * size
    seen = keys >= first
    if diagonal:
        seen = seen & (keys <= places)
    return jnp.where(seen, 0.0, NEG)


def attend(heads, q, kv, bias, state, acc):
    width = heads * HD
    values_t = kv[:, width:].T
    for h in range(heads):
        cut = slice(h * HD, (h + 1) * HD)
        scores = nt(kv[:, cut], q[:, cut]) + bias
        peak = state[h : h + 1, :]
        total = state[heads + h : heads + h + 1, :]
        new_peak = jnp.maximum(peak, jnp.max(scores, axis=0, keepdims=True))
        fade = jnp.exp(peak - new_peak)
        probs = jnp.exp(scores - new_peak)
        state[h : h + 1, :] = new_peak
        state[heads + h : heads + h + 1, :] = total * fade + jnp.sum(probs, axis=0, keepdims=True)
        acc[cut, :] = acc[cut, :] * fade + nn(values_t[cut, :], probs.astype(BF16))


def pack_kernel(heads, scal, *refs):
    weights, vectors, pack = refs[:4], refs[4:13], refs[13]
    holds, sems = refs[14:23], refs[23]
    width = weights[0].shape[0]
    copies = [
        pltpu.make_async_copy(weight, pack.at[pl.ds(i * width, width), :], sems.at[i])
        for i, weight in enumerate(weights)
    ]
    copies += [
        pltpu.make_async_copy(vector, hold, sems.at[4 + i])
        for i, (vector, hold) in enumerate(zip(vectors, holds))
    ]
    for copy in copies:
        copy.start()
    for copy in copies:
        copy.wait()
    lines = [hold[...].reshape(1, hold.shape[0]) for hold in holds[:6]]
    lines = [line.astype(F32) for line in lines]
    for hold in holds[6:]:
        bias = hold[...].astype(F32)
        flat = [bias[h : h + 1, :] for h in range(heads)]
        used = heads * bias.shape[1]
        if used < pack.shape[1]:
            flat.append(jnp.zeros((1, pack.shape[1] - used), F32))
        lines.append(jnp.concatenate(flat, axis=1))
    lines.append(jnp.zeros((16 - len(lines), pack.shape[1]), F32))
    pack[4 * width :, :] = jnp.concatenate(lines, axis=0).astype(BF16)


def first_kernel(heads, seqs, count, scal, tokens, *refs):
    parts, refs = refs[:count], refs[count:]
    full, out_full, vecs, normed, q_out, kv_out, state, acc = refs
    width = heads * HD
    size, model = tokens.shape
    parts = [part[...] for part in parts]
    if count == 2:
        low_first = scal[FSDP] == 0
        parts = [
            jnp.where(low_first, parts[0], parts[1]),
            jnp.where(low_first, parts[1], parts[0]),
        ]
    share = model // count
    full[...] = jnp.concatenate([part[: 3 * width, :share] for part in parts], axis=1)
    out_full[...] = jnp.concatenate(
        [part[3 * width : 4 * width, :share] for part in parts], axis=1
    )
    lines = [part[4 * width :, :].astype(F32) for part in parts]
    vecs[...] = jnp.zeros_like(vecs)
    vecs[0:6, :] = jnp.concatenate([line[0:6, :share] for line in lines], axis=1)
    for row, total in ((6, model), (7, width), (8, width)):
        cut = total // heads // count
        vecs[row : row + 1, :total] = jnp.concatenate(
            [line[row : row + 1, h * cut : (h + 1) * cut] for h in range(heads) for line in lines],
            axis=1,
        )
    xhat, _ = standard(tokens[...].astype(F32))
    low = (xhat * vecs[0:1, :] + vecs[1:2, :]).astype(BF16)
    normed[...] = low
    rows = nt(low, full[...])
    bias = jnp.concatenate(
        [jnp.zeros((1, width), F32), vecs[8:9, :width], vecs[7:8, :width]], axis=1
    )
    rows = (rows + bias).astype(BF16)
    q = rows[:, 2 * width :] * jnp.asarray(HD**-0.5, BF16)
    kv = rows[:, : 2 * width]
    q_out[...] = q
    kv_out[...] = kv
    state[...] = jnp.where(
        lax.broadcasted_iota(jnp.int32, state.shape, 0) < heads, jnp.float32(NEG), 0.0
    )
    acc[...] = jnp.zeros_like(acc)
    mask = mask_bias(scal, seqs, scal[CTX], scal[CTX], size, True)
    attend(heads, q, kv, mask, state, acc)


def others_kernel(heads, seqs, blocks, scal, vecs, full, q, state_in, acc_in, near, far, *refs):
    kvs, refs = refs[: blocks - 1], refs[blocks - 1 :]
    queries, refs = refs[: blocks - 1], refs[blocks - 1 :]
    mixed_t, mix_t, logs, state, acc, tokens = refs
    width = heads * HD
    size = q.shape[0]
    half = size // 2
    side = lax.rem(scal[TP], 2)
    state[...] = state_in[...]
    acc[...] = acc_in[...]

    def normed(block):
        rows = pl.ds(pl.multiple_of(block * half, half), half)
        tokens[pl.ds(pl.multiple_of(side * half, half), half), :] = near[rows, :]
        tokens[pl.ds(pl.multiple_of((1 - side) * half, half), half), :] = far[rows, :]
        xhat, _ = standard(tokens[...].astype(F32))
        return (xhat * vecs[0:1, :] + vecs[1:2, :]).astype(BF16)

    for step in range(1, blocks):
        kv_out, q_out = kvs[step - 1], queries[step - 1]

        @pl.when(scal[CTX] >= step)
        def _():
            block = scal[CTX] - step
            rows = nt(normed(block), full[: 2 * width, :])
            bias = jnp.concatenate([jnp.zeros((1, width), F32), vecs[8:9, :width]], axis=1)
            kv = (rows + bias).astype(BF16)
            kv_out[...] = kv
            mask = mask_bias(scal, seqs, scal[CTX], block, size, False)
            attend(heads, q[...], kv, mask, state, acc)

        @pl.when(scal[CTX] < step)
        def _():
            kv_out[...] = jnp.zeros_like(kv_out)

        @pl.when(scal[CTX] + step < blocks)
        def _():
            rows = nt(normed(scal[CTX] + step), full[2 * width :, :])
            rows = (rows + vecs[7:8, :width]).astype(BF16)
            q_out[...] = rows * jnp.asarray(HD**-0.5, BF16)

        @pl.when(scal[CTX] + step >= blocks)
        def _():
            q_out[...] = jnp.zeros_like(q_out)

    logs[...] = jnp.zeros_like(logs)
    for h in range(heads):
        cut = slice(h * HD, (h + 1) * HD)
        total = state[heads + h : heads + h + 1, :]
        mix = acc[cut, :] / total
        mix_t[cut, :] = mix
        mixed_t[cut, :] = mix.astype(BF16)
        logs[h : h + 1, :] = state[h : h + 1, :] + jnp.log(total)


def mlp_kernel(count, scal, tokens, cotangent, vecs, *refs):
    mixed, refs = refs[:4], refs[4:]
    w_out, refs = refs[0], refs[1:]
    up_parts, refs = refs[:count], refs[count:]
    down_parts, refs = refs[:count], refs[count:]
    (part_out, cot_out, two_out, active_out, grad_out) = refs[:5]
    keep, send1, send2, send3, up, down, back, heads_t = refs[5:]
    index = scal[FSDP]
    place(up, up_parts, index, 0)
    place(down, down_parts, index, 1)
    mid = tokens[...].astype(F32) + vecs[2:3, :]
    width = mixed[0].shape[0]
    for i in range(4):
        slot = jnp.bitwise_xor(scal[TP], i)
        heads_t[pl.ds(pl.multiple_of(slot * width, width), width), :] = mixed[i][...]
    mid = mid + nn(heads_t[...].T, w_out[...])
    back[...] = mid
    size = keep.shape[0]
    own = pl.ds(pl.multiple_of(scal[TP] * size, size), size)
    part_out[...] = back[own, :]
    cot_out[...] = cotangent[own, :]
    xhat, _ = standard(mid)
    two = (xhat * vecs[3:4, :] + vecs[4:5, :]).astype(BF16)
    two_out[...] = two
    v = nn(two, up[...]) + vecs[6:7, :]
    t = jnp.tanh(GELU_C * (v + GELU_A * (v * v * v)))
    active = (0.5 * v * (1.0 + t)).astype(BF16)
    active_out[...] = active
    slope = 0.5 * (1.0 + t) + 0.5 * v * (1.0 - t * t) * (GELU_C * (1.0 + 3.0 * GELU_A * (v * v)))
    grad = (nt(cotangent[...], down[...]) * slope).astype(BF16)
    grad_out[...] = grad
    back[...] = nt(grad, up[...])
    for i, out in enumerate((keep, send1, send2, send3)):
        slot = jnp.bitwise_xor(scal[TP], i)
        out[...] = back[pl.ds(pl.multiple_of(slot * size, size), size), :].astype(out.dtype)


def mid_back_kernel(scal, mid, cotangent, vecs, keep, got1, got2, got3, mid_grad, attn_grad, sums):
    grad = keep[...] + got1[...].astype(F32) + got2[...].astype(F32) + got3[...].astype(F32)
    xhat, scale = standard(mid[...])
    total = cotangent[...].astype(F32) + norm_back(xhat, scale, vecs[3:4, :], grad)
    mid_grad[...] = total
    attn_grad[...] = total.astype(BF16)
    sums[...] = jnp.zeros_like(sums)
    sums[0:1, :] = jnp.sum(grad * xhat, axis=0, keepdims=True)
    sums[1:2, :] = jnp.sum(grad, axis=0, keepdims=True)


def pieces_of(value):
    one = value.astype(BF16).astype(F32)
    two = (value - one).astype(BF16).astype(F32)
    return one, two, value - one - two


def out_back_kernel(heads, scal, w_out, mix_t, logs, part0, part1, part2, part3, rows, pack):
    width = heads * HD
    size = part0.shape[0]
    for i, part in enumerate((part0, part1, part2, part3)):
        slot = jnp.bitwise_xor(scal[TP], i)
        rows[pl.ds(pl.multiple_of(slot * size, size), size), :] = part[...]
    grad_t = nt(w_out[...], rows[...]).astype(BF16)
    pack[:width, :] = grad_t
    wide = grad_t.astype(F32) * mix_t[...]
    stats = [logs[h : h + 1, :] for h in range(heads)]
    stats += [
        jnp.sum(wide[h * HD : (h + 1) * HD, :], axis=0, keepdims=True) for h in range(heads)
    ]
    lines = []
    for stat in stats:
        lines += list(pieces_of(stat))
    lines.append(jnp.zeros((32 - len(lines), rows.shape[0]), F32))
    pack[width:, :] = jnp.concatenate(lines, axis=0).astype(BF16)


def read_stats(heads, pack):
    lines = pack[heads * HD :, :].astype(F32)
    stats = [
        lines[3 * i : 3 * i + 1, :] + lines[3 * i + 1 : 3 * i + 2, :] + lines[3 * i + 2 : 3 * i + 3, :]
        for i in range(2 * heads)
    ]
    return stats[:heads], stats[heads:]


def pair_back(heads, h, q, grad, kv, bias, logs, deltas):
    width = heads * HD
    cut = slice(h * HD, (h + 1) * HD)
    cut_v = slice(width + h * HD, width + (h + 1) * HD)
    probs = jnp.exp(nt(kv[:, cut], q[:, cut]) + bias - logs[h])
    grad_probs = nt(kv[:, cut_v], grad[:, cut])
    return probs.astype(BF16), (probs * (grad_probs - deltas[h])).astype(BF16)


def query_kernel(heads, seqs, count, scal, q, pack, *refs):
    kvs, (dq_out, dq_t_out, acc, dq_t) = refs[:count], refs[count:]
    width = heads * HD
    size = q.shape[0]
    logs, deltas = read_stats(heads, pack)
    grad = pack[:width, :].T
    for step in range(count):

        def work(step=step):
            kv = kvs[step][...]
            keys_t = kv[:, :width].T
            bias = mask_bias(scal, seqs, scal[CTX], scal[CTX] - step, size, step == 0)
            for h in range(heads):
                cut = slice(h * HD, (h + 1) * HD)
                cut_v = slice(width + h * HD, width + (h + 1) * HD)
                probs, grads = pair_back(heads, h, q[...], grad, kv, bias, logs, deltas)
                term = nn(keys_t[cut, :], grads)
                if step == 0:
                    dq_t[cut, :] = term
                    acc[:, cut] = nn(grads, q[:, cut])
                    acc[:, cut_v] = nn(probs, grad[:, cut])
                else:
                    dq_t[cut, :] += term

        if step == 0:
            work()
        else:
            pl.when(scal[CTX] >= step)(work)
    low = (dq_t[...] * (HD**-0.5)).astype(BF16)
    dq_t_out[...] = low
    dq_out[...] = low.T


def key_kernel(heads, seqs, blocks, scal, kv, acc_in, *refs):
    packs, refs = refs[: blocks - 1], refs[blocks - 1 :]
    queries, (out, acc) = refs[: blocks - 1], refs[blocks - 1 :]
    width = heads * HD
    size = kv.shape[0]
    acc[...] = acc_in[...]
    for step in range(1, blocks):

        @pl.when(scal[CTX] + step < blocks)
        def _():
            block = scal[CTX] + step
            pack = packs[step - 1]
            logs, deltas = read_stats(heads, pack)
            grad = pack[:width, :].T
            q = queries[step - 1][...]
            bias = mask_bias(scal, seqs, block, scal[CTX], size, False)
            for h in range(heads):
                cut = slice(h * HD, (h + 1) * HD)
                cut_v = slice(width + h * HD, width + (h + 1) * HD)
                probs, grads = pair_back(heads, h, q, grad, kv[...], bias, logs, deltas)
                acc[:, cut] += nn(grads, q[:, cut])
                acc[:, cut_v] += nn(probs, grad[:, cut])

    out[...] = acc[...].astype(BF16)


def split_store(scal, value, outs):
    if len(outs) == 1:
        outs[0][...] = value
        return
    mine, theirs, hold = outs
    size = mine.shape[1]
    hold[...] = value
    for slot, out in ((scal[FSDP], mine), (1 - scal[FSDP], theirs)):
        out[...] = hold[:, pl.ds(pl.multiple_of(slot * size, size), size)].astype(out.dtype)


def mlp_grads_kernel(scal, active, cotangent, two, grad, sums, *outs):
    each = len(outs) // 2
    split_store(scal, nn(active[...].T, cotangent[...]), outs[:each] + outs[2 * each :])
    split_store(scal, nn(grad[...].T, two[...]), outs[each:])
    sums[...] = jnp.zeros_like(sums)
    sums[0:1, :] = jnp.sum(grad[...].astype(F32), axis=0, keepdims=True)
    sums[1:2, :] = jnp.sum(cotangent[...].astype(F32), axis=0, keepdims=True)


def terms_kernel(count, scal, active, *refs):
    parts, (keep, send1, send2, send3, down, terms) = refs[:count], refs[count:]
    place(down, parts, scal[FSDP], 1)
    terms[...] = nn(active[...], down[...])
    size = keep.shape[0]
    for i, out in enumerate((keep, send1, send2, send3)):
        slot = jnp.bitwise_xor(scal[TP], i)
        out[...] = terms[pl.ds(pl.multiple_of(slot * size, size), size), :].astype(out.dtype)


def layer_kernel(scal, mid, vecs, tokens, keep, got1, got2, got3, out):
    size = keep.shape[0]
    out[:size, :] = tokens[...]
    total = keep[...] + got1[...].astype(F32) + got2[...].astype(F32) + got3[...].astype(F32)
    out[size:, :] = (mid[...] + total + vecs[5:6, :]).astype(BF16)


def proj_grads_kernel(scal, normed, dq_t, dkv, attn_grad, mixed_t, sums, *outs):
    value = [
        nn(dq_t[...], normed[...]),
        nn(mixed_t[...], attn_grad[...]),
        nn(dkv[...].T, normed[...]),
    ]
    split_store(scal, jnp.concatenate(value, axis=0), outs)
    width = dq_t.shape[0]
    sums[...] = jnp.zeros_like(sums)
    sums[0:1, :] = jnp.sum(attn_grad[...].astype(F32), axis=0, keepdims=True)
    column = jnp.sum(dq_t[...].astype(F32), axis=1, keepdims=True)
    sums[1:2, :width] = jnp.broadcast_to(column, (width, 128)).T[0:1, :]
    sums[2:3, :width] = jnp.sum(dkv[:, width:].astype(F32), axis=0, keepdims=True)


def small_kernel(heads, scal, sums_one, sums_mid, sums_proj, sums_mlp, shared, own):
    first = (scal[TP] == 0).astype(F32)
    width = heads * HD
    shared[...] = jnp.concatenate(
        [
            sums_one[0:2, :],
            sums_mid[0:2, :],
            sums_proj[0:1, :] * first,
            sums_mlp[1:2, :] * first,
            jnp.zeros((2, shared.shape[1]), F32),
        ],
        axis=0,
    )
    own[...] = jnp.zeros_like(own)
    own[0:1, :] = sums_mlp[0:1, :]
    own[1:3, :width] = sums_proj[1:3, :width]


def head_back_kernel(scal, full, dq, dkv, keep, send1, send2, send3, back):
    width = dq.shape[1]
    back[...] = nn(dkv[...], full[: 2 * width, :]) + nn(dq[...], full[2 * width :, :])
    size = keep.shape[0]
    for i, out in enumerate((keep, send1, send2, send3)):
        slot = jnp.bitwise_xor(scal[TP], i)
        out[...] = back[pl.ds(pl.multiple_of(slot * size, size), size), :].astype(out.dtype)


def one_back_kernel(scal, tokens, vecs, mid_grad, keep, got1, got2, got3, out, sums):
    size = keep.shape[0]
    rows = pl.ds(pl.multiple_of(scal[TP] * size, size), size)
    grad = keep[...] + got1[...].astype(F32) + got2[...].astype(F32) + got3[...].astype(F32)
    xhat, scale = standard(tokens[rows, :].astype(F32))
    total = mid_grad[...] + norm_back(xhat, scale, vecs[0:1, :], grad)
    out[...] = total.astype(BF16)
    sums[...] = jnp.zeros_like(sums)
    sums[0:1, :] = jnp.sum(grad * xhat, axis=0, keepdims=True)
    sums[1:2, :] = jnp.sum(grad, axis=0, keepdims=True)


def join_kernel(scal, part0, part1, part2, part3, tokens, layer):
    size = part0.shape[0] // 2
    for i, part in enumerate((part0, part1, part2, part3)):
        slot = jnp.bitwise_xor(scal[TP], i)
        rows = pl.ds(pl.multiple_of(slot * size, size), size)
        tokens[rows, :] = part[:size, :].astype(F32)
        layer[rows, :] = part[size:, :]


def spread_kernel(count, scal, small, *refs):
    parts, (keep, send1, send2, send3, rows) = refs[:-5], refs[-5:]
    at = 0
    for i in range(0, len(parts), count):
        value = parts[i][...]
        for part in parts[i + 1 : i + count]:
            value = value + part[...].astype(F32)
        rows[at : at + value.shape[0], :] = value
        at += value.shape[0]
    share = rows.shape[1]
    lines = small.shape[0]
    for i in range(small.shape[1] // share):
        rows[at : at + lines, :] = small[:, i * share : (i + 1) * share]
        at += lines
    if at < rows.shape[0]:
        rows[at:, :] = jnp.zeros((rows.shape[0] - at, share), F32)
    size = keep.shape[0]
    for i, out in enumerate((keep, send1, send2, send3)):
        slot = jnp.bitwise_xor(scal[CTX], i)
        out[...] = rows[pl.ds(pl.multiple_of(slot * size, 16), size), :].astype(out.dtype)


def collect_kernel(owners, scal, part0, part1, part2, part3, *refs):
    (query, out, key, value), vectors, heads, rows = refs[:4], refs[4:10], refs[10:13], refs[13]
    size = part0.shape[0]
    for i, part in enumerate((part0, part1, part2, part3)):
        slot = jnp.bitwise_xor(scal[CTX], i)
        rows[pl.ds(pl.multiple_of(slot * size, 16), size), :] = part[...].astype(F32)
    at = 0
    for result in (query, out, key, value):
        result[...] = rows[at : at + result.shape[0], :]
        at += result.shape[0]
    own = rows[pl.ds(pl.multiple_of(at + scal[FSDP] * 16, 16), 16), :]
    for i, vector in enumerate(vectors):
        vector[...] = own[i]
    lines = [rows[at + 16 * i + 8 : at + 16 * i + 16, :] for i in range(owners)]
    lines = jnp.concatenate(lines, axis=1)
    for i, result in enumerate(heads):
        count, each = result.shape
        for h in range(count):
            line = jnp.zeros((1, each), F32)
            for owner in range(owners):
                first = (h * owners + owner) * each
                found = lines[i : i + 1, first : first + each]
                line = jnp.where(scal[FSDP] == owner, found, line)
            result[h : h + 1, :] = line


def swap_fsdp(value):
    return lax.ppermute(value, "fsdp", [(0, 1), (1, 0)])


def swap_tp(value, bits):
    return lax.ppermute(value, "tp", [(i, i ^ bits) for i in range(4)])


def gather_tp(value):
    far = swap_tp(value, 2)
    near = swap_tp(value, 1)
    return value, near, far, swap_tp(far, 1)


def down_ctx(value, step):
    count = lax.axis_size("ctx")
    return lax.ppermute(value, "ctx", [(i + step, i) for i in range(count - step)])


def chain_one(value):
    part = value.astype(BF16)
    return value, lax.ppermute(part, "ctx", [(0, 1), (3, 2)])


def chain_two(value, got):
    part = (value + got.astype(F32)).astype(BF16)
    return part, lax.ppermute(part, "ctx", [(1, 2), (2, 1)])


def chain_three(part, got):
    part = (part.astype(F32) + got.astype(F32)).astype(BF16)
    return part, lax.ppermute(part, "ctx", [(1, 0), (2, 3)])


def sum_small(shared, own, owners):
    for bits in (1, 2):
        shared = shared + swap_tp(shared, bits)
    both = jnp.concatenate([shared, own], axis=0)
    if owners == 2:
        return both + swap_fsdp(both)
    return lax.psum(both, "fsdp")


def swap_ctx(value, bits):
    return lax.ppermute(value, "ctx", [(i, i ^ bits) for i in range(4)])


def shards(
    tokens,
    g_attn,
    s_attn,
    w_query,
    b_query,
    w_key,
    w_value,
    b_value,
    w_out,
    b_out,
    g_mlp,
    s_mlp,
    w_up,
    b_up,
    w_down,
    b_down,
    cotangent,
    lengths,
):
    owners = lax.axis_size("fsdp")
    blocks = lax.axis_size("ctx")
    pair = owners == 2
    count = 2 if pair else 1
    size, model = tokens.shape
    heads = b_query.shape[0]
    width = heads * HD
    hidden = w_up.shape[1]
    seqs = lengths.shape[1]
    quarter = size // 4
    ctx = lax.axis_index("ctx")
    fsdp = lax.axis_index("fsdp")
    tp = lax.axis_index("tp")
    scal = jnp.concatenate([jnp.stack([ctx, fsdp, tp]).astype(jnp.int32), lengths[0]])

    def fetch(value, axis):
        if pair:
            return (value, swap_fsdp(value))
        return (lax.all_gather(value, "fsdp", axis=axis, tiled=True),)

    share = model // owners
    inner = (ctx == 1) | (ctx == 2)
    lanes = max(share, hidden // owners)
    vectors = (g_attn, s_attn, b_out, g_mlp, s_mlp, b_down, b_up, b_query, b_value)
    anywhere = pl.BlockSpec(memory_space=pl.ANY)
    pack = pl.pallas_call(
        functools.partial(pack_kernel, heads),
        out_shape=shape((4 * width + 16, lanes), BF16),
        in_specs=[pl.BlockSpec(memory_space=pltpu.SMEM)] + [anywhere] * 13,
        out_specs=pl.BlockSpec(memory_space=pltpu.VMEM),
        scratch_shapes=[pltpu.VMEM(vector.shape, BF16) for vector in vectors]
        + [pltpu.SemaphoreType.DMA((13,))],
        name="pack",
    )(scal, w_key.T, w_value.T, w_query.T, w_out, *vectors)
    if pair:
        packs = (pack, swap_fsdp(pack))
    else:
        every = lax.all_gather(pack, "fsdp", axis=0)
        packs = tuple(every[i] for i in range(owners))
    half = lax.dynamic_slice_in_dim(tokens, (tp % 2) * (size // 2), size // 2, 0)
    tokens_near = lax.all_gather(half, "ctx", axis=0, tiled=True)
    up_parts = fetch(after(w_up, packs[-1]), 0)
    down_parts = fetch(after(w_down, up_parts[-1]), 1)

    state_shape = shape((8, size), F32)
    acc_shape = shape((width, size), F32)
    full, out_full, vecs, normed, q, kv, state, acc = call(
        functools.partial(first_kernel, heads, seqs, len(packs)),
        [
            shape((3 * width, model), BF16),
            shape((width, model), BF16),
            shape((16, model), F32),
            shape((size, model), BF16),
            shape((size, width), BF16),
            shape((size, 2 * width), BF16),
            state_shape,
            acc_shape,
        ],
        scal,
        tokens,
        *packs,
        cost=3.5,
        name="attend_first",
    )
    tokens_far = swap_tp(after(tokens_near, state, up_parts[-1]), 1)
    out_all = lax.all_gather(after(out_full, tokens_near), "tp", axis=0, tiled=True)
    *rest, mixed_t, mix_t, logs = call(
        functools.partial(others_kernel, heads, seqs, blocks),
        [shape((size, 2 * width), BF16)] * (blocks - 1)
        + [shape((size, width), BF16)] * (blocks - 1)
        + [shape((width, size), BF16), acc_shape, state_shape],
        scal,
        vecs,
        full,
        q,
        state,
        acc,
        tokens_near,
        tokens_far,
        scratch=[
            pltpu.VMEM((8, size), F32),
            pltpu.VMEM((width, size), F32),
            pltpu.VMEM((size, model), BF16),
        ],
        cost=7.0,
        name="attend_others",
    )
    kvs, upper_q = [kv] + rest[: blocks - 1], rest[blocks - 1 :]

    mixed_parts = gather_tp(mixed_t)
    row_quarter = shape((quarter, model), BF16)
    sent = [shape((quarter, model), F32), row_quarter, row_quarter, row_quarter]
    wide = shape((size, hidden), BF16)
    mid_quarter, cot_quarter, two, active, grad_upper, *back = call(
        functools.partial(mlp_kernel, count),
        [
            shape((quarter, model), F32),
            row_quarter,
            shape((size, model), BF16),
            wide,
            wide,
        ]
        + sent,
        scal,
        tokens,
        cotangent,
        vecs,
        *mixed_parts,
        out_all,
        *up_parts,
        *down_parts,
        scratch=[
            pltpu.VMEM((model, hidden), BF16),
            pltpu.VMEM((hidden, model), BF16),
            pltpu.VMEM((size, model), F32),
            pltpu.VMEM((4 * width, size), BF16),
        ],
        cost=7,
        name="mlp",
    )
    got_mid = [swap_tp(back[i], i) for i in range(1, 4)]

    def grad_outs(lines, held):
        if pair:
            part = (lines, share)
            return [shape(part, F32), shape(part, BF16)], [pltpu.VMEM((held, model), F32)]
        return [shape((lines, model), F32)], []

    def owned(parts):
        if pair:
            return parts[0], swap_fsdp(parts[1])
        return (lax.psum_scatter(parts[0], "fsdp", scatter_dimension=1, tiled=True),)

    def summed(parts):
        return parts[0] + parts[1].astype(F32) if len(parts) == 2 else parts[0]

    sums_shape = shape((8, model), F32)
    outs, scratch = grad_outs(hidden, hidden)
    sums_mlp, *parts = call(
        mlp_grads_kernel,
        [sums_shape] + outs + outs,
        scal,
        after(active, got_mid[0]),
        cotangent,
        two,
        grad_upper,
        scratch=scratch,
        cost=3.2,
        name="mlp_grads",
    )
    own_down = owned(parts[:count])
    mid_grad, attn_quarter, sums_mid = call(
        mid_back_kernel,
        [shape((quarter, model), F32), row_quarter, sums_shape],
        scal,
        mid_quarter,
        cot_quarter,
        after(vecs, sums_mlp),
        back[0],
        *got_mid,
        cost=1.0,
        name="mid_back",
    )
    attn_parts = gather_tp(attn_quarter)
    own_up = owned([after(part, own_down[-1]) for part in parts[count:]])
    one_down = chain_one(summed(own_down))
    attn_grad, pack = call(
        functools.partial(out_back_kernel, heads),
        [shape((size, model), BF16), shape((width + 32, size), BF16)],
        scal,
        after(out_full, own_down[-1]),
        mix_t,
        logs,
        *attn_parts,
        cost=1.1,
        name="out_back",
    )
    upper = [down_ctx(pack, step) for step in range(1, blocks)]
    dq, dq_t, dkv = call(
        functools.partial(query_kernel, heads, seqs, blocks),
        [shape((size, width), BF16), shape((width, size), BF16), shape((size, 2 * width), F32)],
        scal,
        q,
        pack,
        *kvs,
        scratch=[pltpu.VMEM((width, size), F32)],
        cost=5.2,
        name="query_back",
    )
    (dkv,) = call(
        functools.partial(key_kernel, heads, seqs, blocks),
        [shape((size, 2 * width), BF16)],
        scal,
        after(kv, one_down[1]),
        dkv,
        *upper,
        *upper_q,
        scratch=[pltpu.VMEM((size, 2 * width), F32)],
        cost=7.0,
        name="key_back",
    )
    two_down = chain_two(*one_down)
    one_up = chain_one(summed(own_up))
    back = call(
        head_back_kernel,
        sent,
        scal,
        full,
        dq,
        dkv,
        scratch=[pltpu.VMEM((size, model), F32)],
        cost=1.5,
        name="head_back",
    )
    got_one = [swap_tp(back[i], i) for i in range(1, 4)]
    outs, scratch = grad_outs(4 * width, 4 * width)
    sums_proj, *parts = call(
        proj_grads_kernel,
        [sums_shape] + outs,
        scal,
        after(normed, got_one[0]),
        dq_t,
        dkv,
        attn_grad,
        mixed_t,
        scratch=scratch,
        cost=2.5,
        name="proj_grads",
    )
    own_proj = owned(parts)
    terms = call(
        functools.partial(terms_kernel, count),
        sent,
        scal,
        after(active, sums_proj),
        *down_parts,
        scratch=[pltpu.VMEM((hidden, model), BF16), pltpu.VMEM((size, model), F32)],
        cost=1.5,
        name="terms",
    )
    got_terms = [swap_tp(terms[i], i) for i in range(1, 4)]
    token_quarter, sums_one = call(
        one_back_kernel,
        [row_quarter, sums_shape],
        scal,
        tokens,
        vecs,
        after(mid_grad, terms[0], two_down[1], one_up[1]),
        back[0],
        *got_one,
        cost=1.0,
        name="one_back",
    )
    small = call(
        functools.partial(small_kernel, heads),
        [sums_shape, sums_shape],
        scal,
        sums_one,
        sums_mid,
        sums_proj,
        sums_mlp,
        cost=0.6,
        name="small",
    )
    (both,) = call(
        layer_kernel,
        [shape((2 * quarter, model), BF16)],
        scal,
        mid_quarter,
        vecs,
        token_quarter,
        terms[0],
        *got_terms,
        name="layer",
    )
    token_parts = gather_tp(both)
    three_down = chain_three(*two_down)
    two_up = chain_two(*one_up)
    three_up = chain_three(*two_up)
    small = sum_small(*small, owners)
    lines = -(-(4 * width + 16 * owners) // 64) * 64
    piece = shape((lines // 4, share), BF16)
    pieces = call(
        functools.partial(spread_kernel, count),
        [shape((lines // 4, share), F32), piece, piece, piece],
        scal,
        after(small, three_down[1], two_up[1], both),
        *own_proj,
        scratch=[pltpu.VMEM((lines, share), F32)],
        name="spread",
    )
    got = [swap_ctx(pieces[i], i) for i in range(1, 4)]
    piece = (pieces[0] + sum(part.astype(F32) for part in got)).astype(BF16)
    each = shape((width, share), F32)
    vector = shape((share,), F32)
    dw_query, dw_out, dw_key, dw_value, *smalls = call(
        functools.partial(collect_kernel, owners),
        [each] * 4
        + [vector] * 6
        + [shape(bias.shape, F32) for bias in (b_up, b_query, b_value)],
        scal,
        after(piece, three_up[1]),
        *[swap_ctx(piece, i) for i in range(1, 4)],
        scratch=[pltpu.VMEM((lines, share), F32)],
        name="collect",
    )
    d_tokens, layer_out = call(
        join_kernel,
        [shape((size, model), F32), shape((size, model), BF16)],
        scal,
        *token_parts,
        cost=2.0,
        name="join",
    )

    dw_down = jnp.where(inner, *three_down).astype(F32)
    dw_up = jnp.where(inner, *three_up).astype(F32).T
    dg_attn, ds_attn, dg_mlp, ds_mlp, db_out, db_down, db_up, db_query, db_value = smalls
    return (
        layer_out,
        d_tokens,
        dg_attn,
        ds_attn,
        dw_query.T,
        db_query,
        dw_key.T,
        dw_value.T,
        db_value,
        dw_out,
        db_out,
        dg_mlp,
        ds_mlp,
        dw_up,
        db_up,
        dw_down,
        db_down,
    )


def solution(mesh):
    return jax.shard_map(
        shards,
        mesh=mesh,
        in_specs=(
            P(("fsdp", "ctx"), None),
            P("fsdp"),
            P("fsdp"),
            P("fsdp", "tp"),
            P("tp", "fsdp"),
            P("fsdp", "tp"),
            P("fsdp", "tp"),
            P("tp", "fsdp"),
            P("tp", "fsdp"),
            P("fsdp"),
            P("fsdp"),
            P("fsdp"),
            P("fsdp", "tp"),
            P("tp", "fsdp"),
            P("tp", "fsdp"),
            P("fsdp"),
            P(("fsdp", "ctx"), None),
            P("fsdp", None),
        ),
        out_specs=(
            P(("fsdp", "ctx"), None),
            P(("fsdp", "ctx"), None),
            P("fsdp"),
            P("fsdp"),
            P("fsdp", "tp"),
            P("tp", "fsdp"),
            P("fsdp", "tp"),
            P("fsdp", "tp"),
            P("tp", "fsdp"),
            P("tp", "fsdp"),
            P("fsdp"),
            P("fsdp"),
            P("fsdp"),
            P("fsdp", "tp"),
            P("tp", "fsdp"),
            P("tp", "fsdp"),
            P("fsdp"),
        ),
        check_vma=False,
    )
```

```python
import functools

import jax
import jax.numpy as jnp
from jax import lax
from jax.experimental import pallas as pl
from jax.experimental.pallas import tpu as pltpu
from jax.sharding import PartitionSpec as P

HD = 64
BLK = 128
EPS = 1e-05
NEG = -1e30
F32 = jnp.float32
BF16 = jnp.bfloat16
CTX, FSDP, TP, LENGTHS = 0, 1, 2, 3
GELU_C = 0.7978845608028654
GELU_A = 0.044715


def shape(dims, kind):
    return jax.ShapeDtypeStruct(dims, kind)


def call(body, outs, scal, *args, cost=1.0, scratch=(), name=None, staged=False):
    def spec(value):
        if staged:
            return pl.BlockSpec(memory_space=pltpu.VMEM)
        return pl.BlockSpec(value.shape, lambda i: (0,) * len(value.shape))

    return pl.pallas_call(
        body,
        grid=() if staged else (1,),
        out_shape=outs,
        in_specs=[pl.BlockSpec(memory_space=pltpu.SMEM)] + [spec(arg) for arg in args],
        out_specs=[spec(out) for out in outs],
        scratch_shapes=list(scratch),
        compiler_params=pltpu.CompilerParams(vmem_limit_bytes=62 * 1024 * 1024),
        cost_estimate=pl.CostEstimate(
            flops=int(cost * 4e9), bytes_accessed=int(cost * 12e6), transcendentals=0
        ),
        name=name,
    )(scal, *args)


def after(value, *others):
    return lax.optimization_barrier((value,) + others)[0]


def nn(a, b):
    return jnp.dot(a, b, preferred_element_type=F32)


def nt(a, b):
    return lax.dot_general(a, b, (((1,), (1,)), ((), ())), preferred_element_type=F32)


def standard(rows):
    average = jnp.mean(rows, axis=-1, keepdims=True)
    centred = rows - average
    spread = jnp.mean(centred * centred, axis=-1, keepdims=True)
    scale = lax.rsqrt(spread + EPS)
    return centred * scale, scale


def norm_back(xhat, scale, gain, grad):
    e = grad * gain
    return scale * (
        e
        - jnp.mean(e, axis=-1, keepdims=True)
        - xhat * jnp.mean(e * xhat, axis=-1, keepdims=True)
    )


def place(ref, parts, index, axis):
    if len(parts) == 1:
        ref[...] = parts[0][...]
        return
    size = parts[0].shape[axis]
    for part, slot in zip(parts, (index, 1 - index)):
        span = pl.ds(pl.multiple_of(slot * size, size), size)
        if axis == 0:
            ref[span, :] = part[...]
        else:
            ref[:, span] = part[...]


def mask_bias(scal, seqs, query_block, key_block, size, diagonal):
    places = lax.broadcasted_iota(jnp.int32, (1, size), 1) + query_block * size
    first = jnp.zeros((1, size), jnp.int32)
    end = 0
    for i in range(seqs):
        end = end + scal[LENGTHS + i] * BLK
        first = jnp.where(places >= end, end, first)
    keys = lax.broadcasted_iota(jnp.int32, (size, size), 0) + key_block * size
    seen = keys >= first
    if diagonal:
        seen = seen & (keys <= places)
    return jnp.where(seen, 0.0, NEG)


def attend(heads, q, kv, bias, state, acc):
    width = heads * HD
    values_t = kv[:, width:].T
    for h in range(heads):
        cut = slice(h * HD, (h + 1) * HD)
        scores = nt(kv[:, cut], q[:, cut]) + bias
        peak = state[h : h + 1, :]
        total = state[heads + h : heads + h + 1, :]
        new_peak = jnp.maximum(peak, jnp.max(scores, axis=0, keepdims=True))
        fade = jnp.exp(peak - new_peak)
        probs = jnp.exp(scores - new_peak)
        state[h : h + 1, :] = new_peak
        state[heads + h : heads + h + 1, :] = total * fade + jnp.sum(probs, axis=0, keepdims=True)
        acc[cut, :] = acc[cut, :] * fade + nn(values_t[cut, :], probs.astype(BF16))


def pack_kernel(heads, scal, *refs):
    weights, vectors, pack = refs[:4], refs[4:13], refs[13]
    holds, sems = refs[14:23], refs[23]
    width = weights[0].shape[0]
    copies = [
        pltpu.make_async_copy(weight, pack.at[pl.ds(i * width, width), :], sems.at[i])
        for i, weight in enumerate(weights)
    ]
    copies += [
        pltpu.make_async_copy(vector, hold, sems.at[4 + i])
        for i, (vector, hold) in enumerate(zip(vectors, holds))
    ]
    for copy in copies:
        copy.start()
    for copy in copies:
        copy.wait()
    lines = [hold[...].reshape(1, hold.shape[0]) for hold in holds[:6]]
    lines = [line.astype(F32) for line in lines]
    for hold in holds[6:]:
        bias = hold[...].astype(F32)
        flat = [bias[h : h + 1, :] for h in range(heads)]
        used = heads * bias.shape[1]
        if used < pack.shape[1]:
            flat.append(jnp.zeros((1, pack.shape[1] - used), F32))
        lines.append(jnp.concatenate(flat, axis=1))
    lines.append(jnp.zeros((16 - len(lines), pack.shape[1]), F32))
    pack[4 * width :, :] = jnp.concatenate(lines, axis=0).astype(BF16)


def first_kernel(heads, seqs, count, scal, tokens, *refs):
    parts, refs = refs[:count], refs[count:]
    full, out_full, vecs, normed, q_out, kv_out, state, acc = refs
    width = heads * HD
    size, model = tokens.shape
    parts = [part[...] for part in parts]
    if count == 2:
        low_first = scal[FSDP] == 0
        parts = [
            jnp.where(low_first, parts[0], parts[1]),
            jnp.where(low_first, parts[1], parts[0]),
        ]
    share = model // count
    full[...] = jnp.concatenate([part[: 3 * width, :share] for part in parts], axis=1)
    out_full[...] = jnp.concatenate(
        [part[3 * width : 4 * width, :share] for part in parts], axis=1
    )
    lines = [part[4 * width :, :].astype(F32) for part in parts]
    vecs[...] = jnp.zeros_like(vecs)
    vecs[0:6, :] = jnp.concatenate([line[0:6, :share] for line in lines], axis=1)
    for row, total in ((6, model), (7, width), (8, width)):
        cut = total // heads // count
        vecs[row : row + 1, :total] = jnp.concatenate(
            [line[row : row + 1, h * cut : (h + 1) * cut] for h in range(heads) for line in lines],
            axis=1,
        )
    xhat, _ = standard(tokens[...].astype(F32))
    low = (xhat * vecs[0:1, :] + vecs[1:2, :]).astype(BF16)
    normed[...] = low
    rows = nt(low, full[...])
    bias = jnp.concatenate(
        [jnp.zeros((1, width), F32), vecs[8:9, :width], vecs[7:8, :width]], axis=1
    )
    rows = (rows + bias).astype(BF16)
    q = rows[:, 2 * width :] * jnp.asarray(HD**-0.5, BF16)
    kv = rows[:, : 2 * width]
    q_out[...] = q
    kv_out[...] = kv
    state[...] = jnp.where(
        lax.broadcasted_iota(jnp.int32, state.shape, 0) < heads, jnp.float32(NEG), 0.0
    )
    acc[...] = jnp.zeros_like(acc)
    mask = mask_bias(scal, seqs, scal[CTX], scal[CTX], size, True)
    attend(heads, q, kv, mask, state, acc)


def others_kernel(heads, seqs, blocks, scal, vecs, full, q, state_in, acc_in, near, far, *refs):
    kvs, refs = refs[: blocks - 1], refs[blocks - 1 :]
    queries, refs = refs[: blocks - 1], refs[blocks - 1 :]
    mixed_t, mix_t, logs, state, acc, tokens = refs
    width = heads * HD
    size = q.shape[0]
    half = size // 2
    side = lax.rem(scal[TP], 2)
    state[...] = state_in[...]
    acc[...] = acc_in[...]

    def normed(block):
        rows = pl.ds(pl.multiple_of(block * half, half), half)
        tokens[pl.ds(pl.multiple_of(side * half, half), half), :] = near[rows, :]
        tokens[pl.ds(pl.multiple_of((1 - side) * half, half), half), :] = far[rows, :]
        xhat, _ = standard(tokens[...].astype(F32))
        return (xhat * vecs[0:1, :] + vecs[1:2, :]).astype(BF16)

    for step in range(1, blocks):
        kv_out, q_out = kvs[step - 1], queries[step - 1]

        @pl.when(scal[CTX] >= step)
        def _():
            block = scal[CTX] - step
            rows = nt(normed(block), full[: 2 * width, :])
            bias = jnp.concatenate([jnp.zeros((1, width), F32), vecs[8:9, :width]], axis=1)
            kv = (rows + bias).astype(BF16)
            kv_out[...] = kv
            mask = mask_bias(scal, seqs, scal[CTX], block, size, False)
            attend(heads, q[...], kv, mask, state, acc)

        @pl.when(scal[CTX] < step)
        def _():
            kv_out[...] = jnp.zeros_like(kv_out)

        @pl.when(scal[CTX] + step < blocks)
        def _():
            rows = nt(normed(scal[CTX] + step), full[2 * width :, :])
            rows = (rows + vecs[7:8, :width]).astype(BF16)
            q_out[...] = rows * jnp.asarray(HD**-0.5, BF16)

        @pl.when(scal[CTX] + step >= blocks)
        def _():
            q_out[...] = jnp.zeros_like(q_out)

    logs[...] = jnp.zeros_like(logs)
    for h in range(heads):
        cut = slice(h * HD, (h + 1) * HD)
        total = state[heads + h : heads + h + 1, :]
        mix = acc[cut, :] / total
        mix_t[cut, :] = mix
        mixed_t[cut, :] = mix.astype(BF16)
        logs[h : h + 1, :] = state[h : h + 1, :] + jnp.log(total)


def mlp_kernel(count, scal, tokens, cotangent, vecs, *refs):
    mixed, refs = refs[:4], refs[4:]
    w_out, refs = refs[0], refs[1:]
    up_parts, refs = refs[:count], refs[count:]
    down_parts, refs = refs[:count], refs[count:]
    (part_out, cot_out, two_out, active_out, grad_out) = refs[:5]
    keep, send1, send2, send3, up, down, back, heads_t = refs[5:]
    index = scal[FSDP]
    place(up, up_parts, index, 0)
    place(down, down_parts, index, 1)
    mid = tokens[...].astype(F32) + vecs[2:3, :]
    width = mixed[0].shape[0]
    for i in range(4):
        slot = jnp.bitwise_xor(scal[TP], i)
        heads_t[pl.ds(pl.multiple_of(slot * width, width), width), :] = mixed[i][...]
    mid = mid + nn(heads_t[...].T, w_out[...])
    back[...] = mid
    size = keep.shape[0]
    own = pl.ds(pl.multiple_of(scal[TP] * size, size), size)
    part_out[...] = back[own, :]
    cot_out[...] = cotangent[own, :]
    xhat, _ = standard(mid)
    two = (xhat * vecs[3:4, :] + vecs[4:5, :]).astype(BF16)
    two_out[...] = two
    v = nn(two, up[...]) + vecs[6:7, :]
    t = jnp.tanh(GELU_C * (v + GELU_A * (v * v * v)))
    active = (0.5 * v * (1.0 + t)).astype(BF16)
    active_out[...] = active
    slope = 0.5 * (1.0 + t) + 0.5 * v * (1.0 - t * t) * (GELU_C * (1.0 + 3.0 * GELU_A * (v * v)))
    grad = (nt(cotangent[...], down[...]) * slope).astype(BF16)
    grad_out[...] = grad
    back[...] = nt(grad, up[...])
    for i, out in enumerate((keep, send1, send2, send3)):
        slot = jnp.bitwise_xor(scal[TP], i)
        out[...] = back[pl.ds(pl.multiple_of(slot * size, size), size), :].astype(out.dtype)


def mid_back_kernel(scal, mid, cotangent, vecs, keep, got1, got2, got3, mid_grad, attn_grad, sums):
    grad = keep[...] + got1[...].astype(F32) + got2[...].astype(F32) + got3[...].astype(F32)
    xhat, scale = standard(mid[...])
    total = cotangent[...].astype(F32) + norm_back(xhat, scale, vecs[3:4, :], grad)
    mid_grad[...] = total
    attn_grad[...] = total.astype(BF16)
    sums[...] = jnp.zeros_like(sums)
    sums[0:1, :] = jnp.sum(grad * xhat, axis=0, keepdims=True)
    sums[1:2, :] = jnp.sum(grad, axis=0, keepdims=True)


def pieces_of(value):
    one = value.astype(BF16).astype(F32)
    two = (value - one).astype(BF16).astype(F32)
    return one, two, value - one - two


def out_back_kernel(heads, scal, w_out, mix_t, logs, part0, part1, part2, part3, rows, pack):
    width = heads * HD
    size = part0.shape[0]
    for i, part in enumerate((part0, part1, part2, part3)):
        slot = jnp.bitwise_xor(scal[TP], i)
        rows[pl.ds(pl.multiple_of(slot * size, size), size), :] = part[...]
    grad_t = nt(w_out[...], rows[...]).astype(BF16)
    pack[:width, :] = grad_t
    wide = grad_t.astype(F32) * mix_t[...]
    stats = [logs[h : h + 1, :] for h in range(heads)]
    stats += [
        jnp.sum(wide[h * HD : (h + 1) * HD, :], axis=0, keepdims=True) for h in range(heads)
    ]
    lines = []
    for stat in stats:
        lines += list(pieces_of(stat))
    lines.append(jnp.zeros((32 - len(lines), rows.shape[0]), F32))
    pack[width:, :] = jnp.concatenate(lines, axis=0).astype(BF16)


def read_stats(heads, pack):
    lines = pack[heads * HD :, :].astype(F32)
    stats = [
        lines[3 * i : 3 * i + 1, :] + lines[3 * i + 1 : 3 * i + 2, :] + lines[3 * i + 2 : 3 * i + 3, :]
        for i in range(2 * heads)
    ]
    return stats[:heads], stats[heads:]


def pair_back(heads, h, q, grad, kv, bias, logs, deltas):
    width = heads * HD
    cut = slice(h * HD, (h + 1) * HD)
    cut_v = slice(width + h * HD, width + (h + 1) * HD)
    probs = jnp.exp(nt(kv[:, cut], q[:, cut]) + bias - logs[h])
    grad_probs = nt(kv[:, cut_v], grad[:, cut])
    return probs.astype(BF16), (probs * (grad_probs - deltas[h])).astype(BF16)


def query_kernel(heads, seqs, count, scal, q, pack, *refs):
    kvs, (dq_out, dq_t_out, acc, dq_t) = refs[:count], refs[count:]
    width = heads * HD
    size = q.shape[0]
    logs, deltas = read_stats(heads, pack)
    grad = pack[:width, :].T
    for step in range(count):

        def work(step=step):
            kv = kvs[step][...]
            keys_t = kv[:, :width].T
            bias = mask_bias(scal, seqs, scal[CTX], scal[CTX] - step, size, step == 0)
            for h in range(heads):
                cut = slice(h * HD, (h + 1) * HD)
                cut_v = slice(width + h * HD, width + (h + 1) * HD)
                probs, grads = pair_back(heads, h, q[...], grad, kv, bias, logs, deltas)
                term = nn(keys_t[cut, :], grads)
                if step == 0:
                    dq_t[cut, :] = term
                    acc[:, cut] = nn(grads, q[:, cut])
                    acc[:, cut_v] = nn(probs, grad[:, cut])
                else:
                    dq_t[cut, :] += term

        if step == 0:
            work()
        else:
            pl.when(scal[CTX] >= step)(work)
    low = (dq_t[...] * (HD**-0.5)).astype(BF16)
    dq_t_out[...] = low
    dq_out[...] = low.T


def key_kernel(heads, seqs, blocks, scal, kv, acc_in, *refs):
    packs, refs = refs[: blocks - 1], refs[blocks - 1 :]
    queries, (out, acc) = refs[: blocks - 1], refs[blocks - 1 :]
    width = heads * HD
    size = kv.shape[0]
    acc[...] = acc_in[...]
    for step in range(1, blocks):

        @pl.when(scal[CTX] + step < blocks)
        def _():
            block = scal[CTX] + step
            pack = packs[step - 1]
            logs, deltas = read_stats(heads, pack)
            grad = pack[:width, :].T
            q = queries[step - 1][...]
            bias = mask_bias(scal, seqs, block, scal[CTX], size, False)
            for h in range(heads):
                cut = slice(h * HD, (h + 1) * HD)
                cut_v = slice(width + h * HD, width + (h + 1) * HD)
                probs, grads = pair_back(heads, h, q, grad, kv[...], bias, logs, deltas)
                acc[:, cut] += nn(grads, q[:, cut])
                acc[:, cut_v] += nn(probs, grad[:, cut])

    out[...] = acc[...].astype(BF16)


def split_store(scal, value, outs):
    if len(outs) == 1:
        outs[0][...] = value
        return
    mine, theirs, hold = outs
    size = mine.shape[1]
    hold[...] = value
    for slot, out in ((scal[FSDP], mine), (1 - scal[FSDP], theirs)):
        out[...] = hold[:, pl.ds(pl.multiple_of(slot * size, size), size)].astype(out.dtype)


def mlp_grads_kernel(scal, active, cotangent, two, grad, sums, *outs):
    each = len(outs) // 2
    split_store(scal, nn(active[...].T, cotangent[...]), outs[:each] + outs[2 * each :])
    split_store(scal, nn(grad[...].T, two[...]), outs[each:])
    sums[...] = jnp.zeros_like(sums)
    sums[0:1, :] = jnp.sum(grad[...].astype(F32), axis=0, keepdims=True)
    sums[1:2, :] = jnp.sum(cotangent[...].astype(F32), axis=0, keepdims=True)


def terms_kernel(count, scal, active, *refs):
    parts, (keep, send1, send2, send3, down, terms) = refs[:count], refs[count:]
    place(down, parts, scal[FSDP], 1)
    terms[...] = nn(active[...], down[...])
    size = keep.shape[0]
    for i, out in enumerate((keep, send1, send2, send3)):
        slot = jnp.bitwise_xor(scal[TP], i)
        out[...] = terms[pl.ds(pl.multiple_of(slot * size, size), size), :].astype(out.dtype)


def layer_kernel(scal, mid, vecs, tokens, keep, got1, got2, got3, out):
    size = keep.shape[0]
    out[:size, :] = tokens[...]
    total = keep[...] + got1[...].astype(F32) + got2[...].astype(F32) + got3[...].astype(F32)
    out[size:, :] = (mid[...] + total + vecs[5:6, :]).astype(BF16)


def proj_grads_kernel(scal, normed, dq_t, dkv, attn_grad, mixed_t, sums, *outs):
    value = [
        nn(dq_t[...], normed[...]),
        nn(mixed_t[...], attn_grad[...]),
        nn(dkv[...].T, normed[...]),
    ]
    split_store(scal, jnp.concatenate(value, axis=0), outs)
    width = dq_t.shape[0]
    sums[...] = jnp.zeros_like(sums)
    sums[0:1, :] = jnp.sum(attn_grad[...].astype(F32), axis=0, keepdims=True)
    column = jnp.sum(dq_t[...].astype(F32), axis=1, keepdims=True)
    sums[1:2, :width] = jnp.broadcast_to(column, (width, 128)).T[0:1, :]
    sums[2:3, :width] = jnp.sum(dkv[:, width:].astype(F32), axis=0, keepdims=True)


def small_kernel(heads, scal, sums_one, sums_mid, sums_proj, sums_mlp, shared, own):
    first = (scal[TP] == 0).astype(F32)
    width = heads * HD
    shared[...] = jnp.concatenate(
        [
            sums_one[0:2, :],
            sums_mid[0:2, :],
            sums_proj[0:1, :] * first,
            sums_mlp[1:2, :] * first,
            jnp.zeros((2, shared.shape[1]), F32),
        ],
        axis=0,
    )
    own[...] = jnp.zeros_like(own)
    own[0:1, :] = sums_mlp[0:1, :]
    own[1:3, :width] = sums_proj[1:3, :width]


def head_back_kernel(scal, full, dq, dkv, keep, send1, send2, send3, back):
    width = dq.shape[1]
    back[...] = nn(dkv[...], full[: 2 * width, :]) + nn(dq[...], full[2 * width :, :])
    size = keep.shape[0]
    for i, out in enumerate((keep, send1, send2, send3)):
        slot = jnp.bitwise_xor(scal[TP], i)
        out[...] = back[pl.ds(pl.multiple_of(slot * size, size), size), :].astype(out.dtype)


def one_back_kernel(scal, tokens, vecs, mid_grad, keep, got1, got2, got3, out, sums):
    size = keep.shape[0]
    rows = pl.ds(pl.multiple_of(scal[TP] * size, size), size)
    grad = keep[...] + got1[...].astype(F32) + got2[...].astype(F32) + got3[...].astype(F32)
    xhat, scale = standard(tokens[rows, :].astype(F32))
    total = mid_grad[...] + norm_back(xhat, scale, vecs[0:1, :], grad)
    out[...] = total.astype(BF16)
    sums[...] = jnp.zeros_like(sums)
    sums[0:1, :] = jnp.sum(grad * xhat, axis=0, keepdims=True)
    sums[1:2, :] = jnp.sum(grad, axis=0, keepdims=True)


def join_kernel(scal, part0, part1, part2, part3, tokens, layer):
    size = part0.shape[0] // 2
    for i, part in enumerate((part0, part1, part2, part3)):
        slot = jnp.bitwise_xor(scal[TP], i)
        rows = pl.ds(pl.multiple_of(slot * size, size), size)
        tokens[rows, :] = part[:size, :].astype(F32)
        layer[rows, :] = part[size:, :]


def spread_kernel(count, scal, small, *refs):
    parts, (keep, send1, send2, send3, rows) = refs[:-5], refs[-5:]
    at = 0
    for i in range(0, len(parts), count):
        value = parts[i][...]
        for part in parts[i + 1 : i + count]:
            value = value + part[...].astype(F32)
        rows[at : at + value.shape[0], :] = value
        at += value.shape[0]
    share = rows.shape[1]
    lines = small.shape[0]
    for i in range(small.shape[1] // share):
        rows[at : at + lines, :] = small[:, i * share : (i + 1) * share]
        at += lines
    if at < rows.shape[0]:
        rows[at:, :] = jnp.zeros((rows.shape[0] - at, share), F32)
    size = keep.shape[0]
    for i, out in enumerate((keep, send1, send2, send3)):
        slot = jnp.bitwise_xor(scal[CTX], i)
        out[...] = rows[pl.ds(pl.multiple_of(slot * size, 16), size), :].astype(out.dtype)


def collect_kernel(owners, scal, part0, part1, part2, part3, *refs):
    (query, out, key, value), vectors, heads, rows = refs[:4], refs[4:10], refs[10:13], refs[13]
    size = part0.shape[0]
    for i, part in enumerate((part0, part1, part2, part3)):
        slot = jnp.bitwise_xor(scal[CTX], i)
        rows[pl.ds(pl.multiple_of(slot * size, 16), size), :] = part[...].astype(F32)
    at = 0
    for result in (query, out, key, value):
        result[...] = rows[at : at + result.shape[0], :]
        at += result.shape[0]
    own = rows[pl.ds(pl.multiple_of(at + scal[FSDP] * 16, 16), 16), :]
    for i, vector in enumerate(vectors):
        vector[...] = own[i]
    lines = [rows[at + 16 * i + 8 : at + 16 * i + 16, :] for i in range(owners)]
    lines = jnp.concatenate(lines, axis=1)
    for i, result in enumerate(heads):
        count, each = result.shape
        for h in range(count):
            line = jnp.zeros((1, each), F32)
            for owner in range(owners):
                first = (h * owners + owner) * each
                found = lines[i : i + 1, first : first + each]
                line = jnp.where(scal[FSDP] == owner, found, line)
            result[h : h + 1, :] = line


def swap_fsdp(value):
    return lax.ppermute(value, "fsdp", [(0, 1), (1, 0)])


def swap_tp(value, bits):
    return lax.ppermute(value, "tp", [(i, i ^ bits) for i in range(4)])


def gather_tp(value):
    far = swap_tp(value, 2)
    near = swap_tp(value, 1)
    return value, near, far, swap_tp(far, 1)


def down_ctx(value, step):
    count = lax.axis_size("ctx")
    return lax.ppermute(value, "ctx", [(i + step, i) for i in range(count - step)])


def chain_one(value):
    part = value.astype(BF16)
    return part, lax.ppermute(part, "ctx", [(0, 1), (3, 2)])


def chain_two(part, got):
    part = (part.astype(F32) + got.astype(F32)).astype(BF16)
    return part, lax.ppermute(part, "ctx", [(1, 2), (2, 1)])


def chain_three(part, got):
    part = (part.astype(F32) + got.astype(F32)).astype(BF16)
    return part, lax.ppermute(part, "ctx", [(1, 0), (2, 3)])


def sum_small(shared, own, owners, other):
    for bits in (1, 2):
        shared = shared + swap_tp(shared, bits)
    both = after(jnp.concatenate([shared, own], axis=0), other)
    if owners == 2:
        return both + swap_fsdp(both)
    return lax.psum(both, "fsdp")


def swap_ctx(value, bits):
    return lax.ppermute(value, "ctx", [(i, i ^ bits) for i in range(4)])


def shards(
    tokens,
    g_attn,
    s_attn,
    w_query,
    b_query,
    w_key,
    w_value,
    b_value,
    w_out,
    b_out,
    g_mlp,
    s_mlp,
    w_up,
    b_up,
    w_down,
    b_down,
    cotangent,
    lengths,
):
    owners = lax.axis_size("fsdp")
    blocks = lax.axis_size("ctx")
    pair = owners == 2
    count = 2 if pair else 1
    size, model = tokens.shape
    heads = b_query.shape[0]
    width = heads * HD
    hidden = w_up.shape[1]
    seqs = lengths.shape[1]
    quarter = size // 4
    ctx = lax.axis_index("ctx")
    fsdp = lax.axis_index("fsdp")
    tp = lax.axis_index("tp")
    scal = jnp.concatenate([jnp.stack([ctx, fsdp, tp]).astype(jnp.int32), lengths[0]])

    def fetch(value, axis):
        if pair:
            return (value, swap_fsdp(value))
        return (lax.all_gather(value, "fsdp", axis=axis, tiled=True),)

    share = model // owners
    inner = (ctx == 1) | (ctx == 2)
    lanes = max(share, hidden // owners)
    vectors = (g_attn, s_attn, b_out, g_mlp, s_mlp, b_down, b_up, b_query, b_value)
    anywhere = pl.BlockSpec(memory_space=pl.ANY)
    pack = pl.pallas_call(
        functools.partial(pack_kernel, heads),
        out_shape=shape((4 * width + 16, lanes), BF16),
        in_specs=[pl.BlockSpec(memory_space=pltpu.SMEM)] + [anywhere] * 13,
        out_specs=pl.BlockSpec(memory_space=pltpu.VMEM),
        scratch_shapes=[pltpu.VMEM(vector.shape, BF16) for vector in vectors]
        + [pltpu.SemaphoreType.DMA((13,))],
        name="pack",
    )(scal, w_key.T, w_value.T, w_query.T, w_out, *vectors)
    if pair:
        packs = (pack, swap_fsdp(pack))
    else:
        every = lax.all_gather(pack, "fsdp", axis=0)
        packs = tuple(every[i] for i in range(owners))
    half = lax.dynamic_slice_in_dim(tokens, (tp % 2) * (size // 2), size // 2, 0)
    tokens_near = lax.all_gather(half, "ctx", axis=0, tiled=True)
    up_parts = fetch(after(w_up, packs[-1]), 0)
    down_parts = fetch(after(w_down, up_parts[-1]), 1)

    state_shape = shape((8, size), F32)
    acc_shape = shape((width, size), F32)
    full, out_full, vecs, normed, q, kv, state, acc = call(
        functools.partial(first_kernel, heads, seqs, len(packs)),
        [
            shape((3 * width, model), BF16),
            shape((width, model), BF16),
            shape((16, model), F32),
            shape((size, model), BF16),
            shape((size, width), BF16),
            shape((size, 2 * width), BF16),
            state_shape,
            acc_shape,
        ],
        scal,
        tokens,
        *packs,
        cost=3.5,
        name="attend_first",
    )
    tokens_far = swap_tp(after(tokens_near, state, up_parts[-1]), 1)
    out_all = lax.all_gather(after(out_full, tokens_near), "tp", axis=0, tiled=True)
    *rest, mixed_t, mix_t, logs = call(
        functools.partial(others_kernel, heads, seqs, blocks),
        [shape((size, 2 * width), BF16)] * (blocks - 1)
        + [shape((size, width), BF16)] * (blocks - 1)
        + [shape((width, size), BF16), acc_shape, state_shape],
        scal,
        vecs,
        full,
        q,
        state,
        acc,
        tokens_near,
        tokens_far,
        scratch=[
            pltpu.VMEM((8, size), F32),
            pltpu.VMEM((width, size), F32),
            pltpu.VMEM((size, model), BF16),
        ],
        cost=7.0,
        name="attend_others",
    )
    kvs, upper_q = [kv] + rest[: blocks - 1], rest[blocks - 1 :]

    mixed_parts = gather_tp(mixed_t)
    row_quarter = shape((quarter, model), BF16)
    sent = [shape((quarter, model), F32), row_quarter, row_quarter, row_quarter]
    wide = shape((size, hidden), BF16)
    mid_quarter, cot_quarter, two, active, grad_upper, *back = call(
        functools.partial(mlp_kernel, count),
        [
            shape((quarter, model), F32),
            row_quarter,
            shape((size, model), BF16),
            wide,
            wide,
        ]
        + sent,
        scal,
        tokens,
        cotangent,
        vecs,
        *mixed_parts,
        out_all,
        *up_parts,
        *down_parts,
        scratch=[
            pltpu.VMEM((model, hidden), BF16),
            pltpu.VMEM((hidden, model), BF16),
            pltpu.VMEM((size, model), F32),
            pltpu.VMEM((4 * width, size), BF16),
        ],
        cost=7,
        name="mlp",
    )
    got_mid = [swap_tp(back[i], i) for i in range(1, 4)]

    def grad_outs(lines, held):
        if pair:
            part = (lines, share)
            return [shape(part, F32), shape(part, BF16)], [pltpu.VMEM((held, model), F32)]
        return [shape((lines, model), F32)], []

    def owned(parts):
        if pair:
            return parts[0], swap_fsdp(parts[1])
        return (lax.psum_scatter(parts[0], "fsdp", scatter_dimension=1, tiled=True),)

    def summed(parts):
        return parts[0] + parts[1].astype(F32) if len(parts) == 2 else parts[0]

    sums_shape = shape((8, model), F32)
    outs, scratch = grad_outs(hidden, hidden)
    sums_mlp, *parts = call(
        mlp_grads_kernel,
        [sums_shape] + outs + outs,
        scal,
        after(active, got_mid[0]),
        cotangent,
        two,
        grad_upper,
        scratch=scratch,
        cost=3.2,
        name="mlp_grads",
    )
    own_down = owned(parts[:count])
    mid_grad, attn_quarter, sums_mid = call(
        mid_back_kernel,
        [shape((quarter, model), F32), row_quarter, sums_shape],
        scal,
        mid_quarter,
        cot_quarter,
        after(vecs, sums_mlp),
        back[0],
        *got_mid,
        cost=1.0,
        name="mid_back",
    )
    attn_parts = gather_tp(attn_quarter)
    own_up = owned([after(part, own_down[-1]) for part in parts[count:]])
    one_down = chain_one(summed(own_down))
    attn_grad, pack = call(
        functools.partial(out_back_kernel, heads),
        [shape((size, model), BF16), shape((width + 32, size), BF16)],
        scal,
        after(out_full, own_down[-1]),
        mix_t,
        logs,
        *attn_parts,
        cost=1.1,
        name="out_back",
    )
    upper = [down_ctx(pack, step) for step in range(1, blocks)]
    dq, dq_t, dkv = call(
        functools.partial(query_kernel, heads, seqs, blocks),
        [shape((size, width), BF16), shape((width, size), BF16), shape((size, 2 * width), F32)],
        scal,
        q,
        pack,
        *kvs,
        scratch=[pltpu.VMEM((width, size), F32)],
        cost=5.2,
        name="query_back",
    )
    (dkv,) = call(
        functools.partial(key_kernel, heads, seqs, blocks),
        [shape((size, 2 * width), BF16)],
        scal,
        kv,
        dkv,
        *upper,
        *upper_q,
        scratch=[pltpu.VMEM((size, 2 * width), F32)],
        cost=7.0,
        name="key_back",
    )
    two_down = chain_two(*one_down)
    one_up = chain_one(summed(own_up))
    back = call(
        head_back_kernel,
        sent,
        scal,
        full,
        dq,
        after(dkv, one_down[1]),
        scratch=[pltpu.VMEM((size, model), F32)],
        cost=1.5,
        name="head_back",
    )
    got_one = [swap_tp(back[i], i) for i in range(1, 4)]
    outs, scratch = grad_outs(4 * width, 4 * width)
    sums_proj, *parts = call(
        proj_grads_kernel,
        [sums_shape] + outs,
        scal,
        after(normed, got_one[0]),
        dq_t,
        dkv,
        attn_grad,
        mixed_t,
        scratch=scratch,
        cost=2.5,
        name="proj_grads",
    )
    own_proj = owned(parts)
    terms = call(
        functools.partial(terms_kernel, count),
        sent,
        scal,
        after(active, sums_proj),
        *down_parts,
        scratch=[pltpu.VMEM((hidden, model), BF16), pltpu.VMEM((size, model), F32)],
        cost=1.5,
        name="terms",
    )
    got_terms = [swap_tp(terms[i], i) for i in range(1, 4)]
    token_quarter, sums_one = call(
        one_back_kernel,
        [row_quarter, sums_shape],
        scal,
        tokens,
        vecs,
        after(mid_grad, terms[0]),
        back[0],
        *got_one,
        cost=1.0,
        name="one_back",
    )
    small = call(
        functools.partial(small_kernel, heads),
        [sums_shape, sums_shape],
        scal,
        after(sums_one, two_down[1], one_up[1]),
        sums_mid,
        sums_proj,
        sums_mlp,
        cost=0.6,
        name="small",
    )
    (both,) = call(
        layer_kernel,
        [shape((2 * quarter, model), BF16)],
        scal,
        mid_quarter,
        vecs,
        token_quarter,
        terms[0],
        *got_terms,
        name="layer",
    )
    token_parts = gather_tp(both)
    three_down = chain_three(*two_down)
    two_up = chain_two(*one_up)
    three_up = chain_three(*two_up)
    small = sum_small(*small, owners, own_proj[-1])
    lines = -(-(4 * width + 16 * owners) // 64) * 64
    piece = shape((lines // 4, share), BF16)
    pieces = call(
        functools.partial(spread_kernel, count),
        [shape((lines // 4, share), F32), piece, piece, piece],
        scal,
        after(small, two_down[1], one_up[1]),
        *own_proj,
        scratch=[pltpu.VMEM((lines, share), F32)],
        name="spread",
    )
    got = [swap_ctx(pieces[i], i) for i in range(1, 4)]
    piece = (pieces[0] + sum(part.astype(F32) for part in got)).astype(BF16)
    piece = after(piece, three_down[1], two_up[1])
    each = shape((width, share), F32)
    vector = shape((share,), F32)
    dw_query, dw_out, dw_key, dw_value, *smalls = call(
        functools.partial(collect_kernel, owners),
        [each] * 4
        + [vector] * 6
        + [shape(bias.shape, F32) for bias in (b_up, b_query, b_value)],
        scal,
        piece,
        *[swap_ctx(piece, i) for i in range(1, 4)],
        scratch=[pltpu.VMEM((lines, share), F32)],
        name="collect",
    )
    d_tokens, layer_out = call(
        join_kernel,
        [shape((size, model), F32), shape((size, model), BF16)],
        scal,
        *token_parts,
        cost=2.0,
        name="join",
    )

    dw_down = jnp.where(inner, *three_down).astype(F32)
    dw_up = jnp.where(inner, *three_up).astype(F32).T
    dg_attn, ds_attn, dg_mlp, ds_mlp, db_out, db_down, db_up, db_query, db_value = smalls
    return (
        layer_out,
        d_tokens,
        dg_attn,
        ds_attn,
        dw_query.T,
        db_query,
        dw_key.T,
        dw_value.T,
        db_value,
        dw_out,
        db_out,
        dg_mlp,
        ds_mlp,
        dw_up,
        db_up,
        dw_down,
        db_down,
    )


def solution(mesh):
    return jax.shard_map(
        shards,
        mesh=mesh,
        in_specs=(
            P(("fsdp", "ctx"), None),
            P("fsdp"),
            P("fsdp"),
            P("fsdp", "tp"),
            P("tp", "fsdp"),
            P("fsdp", "tp"),
            P("fsdp", "tp"),
            P("tp", "fsdp"),
            P("tp", "fsdp"),
            P("fsdp"),
            P("fsdp"),
            P("fsdp"),
            P("fsdp", "tp"),
            P("tp", "fsdp"),
            P("tp", "fsdp"),
            P("fsdp"),
            P(("fsdp", "ctx"), None),
            P("fsdp", None),
        ),
        out_specs=(
            P(("fsdp", "ctx"), None),
            P(("fsdp", "ctx"), None),
            P("fsdp"),
            P("fsdp"),
            P("fsdp", "tp"),
            P("tp", "fsdp"),
            P("fsdp", "tp"),
            P("fsdp", "tp"),
            P("tp", "fsdp"),
            P("tp", "fsdp"),
            P("fsdp"),
            P("fsdp"),
            P("fsdp"),
            P("fsdp", "tp"),
            P("tp", "fsdp"),
            P("tp", "fsdp"),
            P("fsdp"),
        ),
        check_vma=False,
    )
```

```python
import functools

import jax
import jax.numpy as jnp
from jax import lax
from jax.experimental import pallas as pl
from jax.experimental.pallas import tpu as pltpu
from jax.sharding import PartitionSpec as P

HD = 64
BLK = 128
EPS = 1e-05
NEG = -1e30
F32 = jnp.float32
BF16 = jnp.bfloat16
CTX, FSDP, TP, LENGTHS = 0, 1, 2, 3
GELU_C = 0.7978845608028654
GELU_A = 0.044715


def shape(dims, kind):
    return jax.ShapeDtypeStruct(dims, kind)


def call(body, outs, scal, *args, cost=1.0, scratch=(), name=None, staged=False):
    def spec(value):
        if staged:
            return pl.BlockSpec(memory_space=pltpu.VMEM)
        return pl.BlockSpec(value.shape, lambda i: (0,) * len(value.shape))

    return pl.pallas_call(
        body,
        grid=() if staged else (1,),
        out_shape=outs,
        in_specs=[pl.BlockSpec(memory_space=pltpu.SMEM)] + [spec(arg) for arg in args],
        out_specs=[spec(out) for out in outs],
        scratch_shapes=list(scratch),
        compiler_params=pltpu.CompilerParams(vmem_limit_bytes=62 * 1024 * 1024),
        cost_estimate=pl.CostEstimate(
            flops=int(cost * 4e9), bytes_accessed=int(cost * 12e6), transcendentals=0
        ),
        name=name,
    )(scal, *args)


def after(value, *others):
    return lax.optimization_barrier((value,) + others)[0]


def nn(a, b):
    return jnp.dot(a, b, preferred_element_type=F32)


def nt(a, b):
    return lax.dot_general(a, b, (((1,), (1,)), ((), ())), preferred_element_type=F32)


def standard(rows):
    average = jnp.mean(rows, axis=-1, keepdims=True)
    centred = rows - average
    spread = jnp.mean(centred * centred, axis=-1, keepdims=True)
    scale = lax.rsqrt(spread + EPS)
    return centred * scale, scale


def norm_back(xhat, scale, gain, grad):
    e = grad * gain
    return scale * (
        e
        - jnp.mean(e, axis=-1, keepdims=True)
        - xhat * jnp.mean(e * xhat, axis=-1, keepdims=True)
    )


def place(ref, parts, index, axis):
    if len(parts) == 1:
        ref[...] = parts[0][...]
        return
    size = parts[0].shape[axis]
    for part, slot in zip(parts, (index, 1 - index)):
        span = pl.ds(pl.multiple_of(slot * size, size), size)
        if axis == 0:
            ref[span, :] = part[...]
        else:
            ref[:, span] = part[...]


def mask_bias(scal, seqs, query_block, key_block, size, diagonal):
    places = lax.broadcasted_iota(jnp.int32, (1, size), 1) + query_block * size
    first = jnp.zeros((1, size), jnp.int32)
    end = 0
    for i in range(seqs):
        end = end + scal[LENGTHS + i] * BLK
        first = jnp.where(places >= end, end, first)
    keys = lax.broadcasted_iota(jnp.int32, (size, size), 0) + key_block * size
    seen = keys >= first
    if diagonal:
        seen = seen & (keys <= places)
    return jnp.where(seen, 0.0, NEG)


def attend(heads, q, kv, bias, state, acc):
    width = heads * HD
    values_t = kv[:, width:].T
    for h in range(heads):
        cut = slice(h * HD, (h + 1) * HD)
        scores = nt(kv[:, cut], q[:, cut]) + bias
        peak = state[h : h + 1, :]
        total = state[heads + h : heads + h + 1, :]
        new_peak = jnp.maximum(peak, jnp.max(scores, axis=0, keepdims=True))
        fade = jnp.exp(peak - new_peak)
        probs = jnp.exp(scores - new_peak)
        state[h : h + 1, :] = new_peak
        state[heads + h : heads + h + 1, :] = total * fade + jnp.sum(probs, axis=0, keepdims=True)
        acc[cut, :] = acc[cut, :] * fade + nn(values_t[cut, :], probs.astype(BF16))


def pack_kernel(heads, scal, *refs):
    weights, vectors, pack = refs[:4], refs[4:13], refs[13]
    holds, sems = refs[14:23], refs[23]
    width = weights[0].shape[0]
    copies = [
        pltpu.make_async_copy(weight, pack.at[pl.ds(i * width, width), :], sems.at[i])
        for i, weight in enumerate(weights)
    ]
    copies += [
        pltpu.make_async_copy(vector, hold, sems.at[4 + i])
        for i, (vector, hold) in enumerate(zip(vectors, holds))
    ]
    for copy in copies:
        copy.start()
    for copy in copies:
        copy.wait()
    lines = [hold[...].reshape(1, hold.shape[0]) for hold in holds[:6]]
    lines = [line.astype(F32) for line in lines]
    for hold in holds[6:]:
        bias = hold[...].astype(F32)
        flat = [bias[h : h + 1, :] for h in range(heads)]
        used = heads * bias.shape[1]
        if used < pack.shape[1]:
            flat.append(jnp.zeros((1, pack.shape[1] - used), F32))
        lines.append(jnp.concatenate(flat, axis=1))
    lines.append(jnp.zeros((16 - len(lines), pack.shape[1]), F32))
    pack[4 * width :, :] = jnp.concatenate(lines, axis=0).astype(BF16)


def first_kernel(heads, seqs, count, scal, tokens, *refs):
    parts, refs = refs[:count], refs[count:]
    full, out_full, vecs, normed, q_out, kv_out, state, acc = refs
    width = heads * HD
    size, model = tokens.shape
    parts = [part[...] for part in parts]
    if count == 2:
        low_first = scal[FSDP] == 0
        parts = [
            jnp.where(low_first, parts[0], parts[1]),
            jnp.where(low_first, parts[1], parts[0]),
        ]
    share = model // count
    full[...] = jnp.concatenate([part[: 3 * width, :share] for part in parts], axis=1)
    out_full[...] = jnp.concatenate(
        [part[3 * width : 4 * width, :share] for part in parts], axis=1
    )
    lines = [part[4 * width :, :].astype(F32) for part in parts]
    vecs[...] = jnp.zeros_like(vecs)
    vecs[0:6, :] = jnp.concatenate([line[0:6, :share] for line in lines], axis=1)
    for row, total in ((6, model), (7, width), (8, width)):
        cut = total // heads // count
        vecs[row : row + 1, :total] = jnp.concatenate(
            [line[row : row + 1, h * cut : (h + 1) * cut] for h in range(heads) for line in lines],
            axis=1,
        )
    xhat, _ = standard(tokens[...].astype(F32))
    low = (xhat * vecs[0:1, :] + vecs[1:2, :]).astype(BF16)
    normed[...] = low
    rows = nt(low, full[...])
    bias = jnp.concatenate(
        [jnp.zeros((1, width), F32), vecs[8:9, :width], vecs[7:8, :width]], axis=1
    )
    rows = (rows + bias).astype(BF16)
    q = rows[:, 2 * width :] * jnp.asarray(HD**-0.5, BF16)
    kv = rows[:, : 2 * width]
    q_out[...] = q
    kv_out[...] = kv
    state[...] = jnp.where(
        lax.broadcasted_iota(jnp.int32, state.shape, 0) < heads, jnp.float32(NEG), 0.0
    )
    acc[...] = jnp.zeros_like(acc)
    mask = mask_bias(scal, seqs, scal[CTX], scal[CTX], size, True)
    attend(heads, q, kv, mask, state, acc)


def others_kernel(heads, seqs, blocks, scal, vecs, full, q, state_in, acc_in, near, far, *refs):
    kvs, refs = refs[: blocks - 1], refs[blocks - 1 :]
    queries, refs = refs[: blocks - 1], refs[blocks - 1 :]
    mixed_t, mix_t, logs, state, acc, tokens = refs
    width = heads * HD
    size = q.shape[0]
    half = size // 2
    side = lax.rem(scal[TP], 2)
    state[...] = state_in[...]
    acc[...] = acc_in[...]

    def normed(block):
        rows = pl.ds(pl.multiple_of(block * half, half), half)
        tokens[pl.ds(pl.multiple_of(side * half, half), half), :] = near[rows, :]
        tokens[pl.ds(pl.multiple_of((1 - side) * half, half), half), :] = far[rows, :]
        xhat, _ = standard(tokens[...].astype(F32))
        return (xhat * vecs[0:1, :] + vecs[1:2, :]).astype(BF16)

    for step in range(1, blocks):
        kv_out, q_out = kvs[step - 1], queries[step - 1]

        @pl.when(scal[CTX] >= step)
        def _():
            block = scal[CTX] - step
            rows = nt(normed(block), full[: 2 * width, :])
            bias = jnp.concatenate([jnp.zeros((1, width), F32), vecs[8:9, :width]], axis=1)
            kv = (rows + bias).astype(BF16)
            kv_out[...] = kv
            mask = mask_bias(scal, seqs, scal[CTX], block, size, False)
            attend(heads, q[...], kv, mask, state, acc)

        @pl.when(scal[CTX] < step)
        def _():
            kv_out[...] = jnp.zeros_like(kv_out)

        @pl.when(scal[CTX] + step < blocks)
        def _():
            rows = nt(normed(scal[CTX] + step), full[2 * width :, :])
            rows = (rows + vecs[7:8, :width]).astype(BF16)
            q_out[...] = rows * jnp.asarray(HD**-0.5, BF16)

        @pl.when(scal[CTX] + step >= blocks)
        def _():
            q_out[...] = jnp.zeros_like(q_out)

    logs[...] = jnp.zeros_like(logs)
    for h in range(heads):
        cut = slice(h * HD, (h + 1) * HD)
        total = state[heads + h : heads + h + 1, :]
        mix = acc[cut, :] / total
        mix_t[cut, :] = mix
        mixed_t[cut, :] = mix.astype(BF16)
        logs[h : h + 1, :] = state[h : h + 1, :] + jnp.log(total)


def mlp_kernel(count, scal, tokens, cotangent, vecs, *refs):
    mixed, refs = refs[:4], refs[4:]
    w_out, refs = refs[0], refs[1:]
    up_parts, refs = refs[:count], refs[count:]
    down_parts, refs = refs[:count], refs[count:]
    (part_out, cot_out, two_out, active_out, grad_out) = refs[:5]
    keep, send1, send2, send3, up, down, back, heads_t = refs[5:]
    index = scal[FSDP]
    place(up, up_parts, index, 0)
    place(down, down_parts, index, 1)
    mid = tokens[...].astype(F32) + vecs[2:3, :]
    width = mixed[0].shape[0]
    for i in range(4):
        slot = jnp.bitwise_xor(scal[TP], i)
        heads_t[pl.ds(pl.multiple_of(slot * width, width), width), :] = mixed[i][...]
    mid = mid + nn(heads_t[...].T, w_out[...])
    back[...] = mid
    size = keep.shape[0]
    own = pl.ds(pl.multiple_of(scal[TP] * size, size), size)
    part_out[...] = back[own, :]
    cot_out[...] = cotangent[own, :]
    xhat, _ = standard(mid)
    two = (xhat * vecs[3:4, :] + vecs[4:5, :]).astype(BF16)
    two_out[...] = two
    v = nn(two, up[...]) + vecs[6:7, :]
    t = jnp.tanh(GELU_C * (v + GELU_A * (v * v * v)))
    active = (0.5 * v * (1.0 + t)).astype(BF16)
    active_out[...] = active
    slope = 0.5 * (1.0 + t) + 0.5 * v * (1.0 - t * t) * (GELU_C * (1.0 + 3.0 * GELU_A * (v * v)))
    grad = (nt(cotangent[...], down[...]) * slope).astype(BF16)
    grad_out[...] = grad
    back[...] = nt(grad, up[...])
    for i, out in enumerate((keep, send1, send2, send3)):
        slot = jnp.bitwise_xor(scal[TP], i)
        out[...] = back[pl.ds(pl.multiple_of(slot * size, size), size), :].astype(out.dtype)


def mid_back_kernel(scal, mid, cotangent, vecs, keep, got1, got2, got3, mid_grad, attn_grad, sums):
    grad = keep[...] + got1[...].astype(F32) + got2[...].astype(F32) + got3[...].astype(F32)
    xhat, scale = standard(mid[...])
    total = cotangent[...].astype(F32) + norm_back(xhat, scale, vecs[3:4, :], grad)
    mid_grad[...] = total
    attn_grad[...] = total.astype(BF16)
    sums[...] = jnp.zeros_like(sums)
    sums[0:1, :] = jnp.sum(grad * xhat, axis=0, keepdims=True)
    sums[1:2, :] = jnp.sum(grad, axis=0, keepdims=True)


def pieces_of(value):
    one = value.astype(BF16).astype(F32)
    two = (value - one).astype(BF16).astype(F32)
    return one, two, value - one - two


def out_back_kernel(heads, scal, w_out, mix_t, logs, part0, part1, part2, part3, rows, pack):
    width = heads * HD
    size = part0.shape[0]
    for i, part in enumerate((part0, part1, part2, part3)):
        slot = jnp.bitwise_xor(scal[TP], i)
        rows[pl.ds(pl.multiple_of(slot * size, size), size), :] = part[...]
    grad_t = nt(w_out[...], rows[...]).astype(BF16)
    pack[:width, :] = grad_t
    wide = grad_t.astype(F32) * mix_t[...]
    stats = [logs[h : h + 1, :] for h in range(heads)]
    stats += [
        jnp.sum(wide[h * HD : (h + 1) * HD, :], axis=0, keepdims=True) for h in range(heads)
    ]
    lines = []
    for stat in stats:
        lines += list(pieces_of(stat))
    lines.append(jnp.zeros((32 - len(lines), rows.shape[0]), F32))
    pack[width:, :] = jnp.concatenate(lines, axis=0).astype(BF16)


def read_stats(heads, pack):
    lines = pack[heads * HD :, :].astype(F32)
    stats = [
        lines[3 * i : 3 * i + 1, :] + lines[3 * i + 1 : 3 * i + 2, :] + lines[3 * i + 2 : 3 * i + 3, :]
        for i in range(2 * heads)
    ]
    return stats[:heads], stats[heads:]


def pair_back(heads, h, q, grad, kv, bias, logs, deltas):
    width = heads * HD
    cut = slice(h * HD, (h + 1) * HD)
    cut_v = slice(width + h * HD, width + (h + 1) * HD)
    probs = jnp.exp(nt(kv[:, cut], q[:, cut]) + bias - logs[h])
    grad_probs = nt(kv[:, cut_v], grad[:, cut])
    return probs.astype(BF16), (probs * (grad_probs - deltas[h])).astype(BF16)


def query_kernel(heads, seqs, count, scal, q, pack, *refs):
    kvs, (dq_out, dq_t_out, acc, dq_t) = refs[:count], refs[count:]
    width = heads * HD
    size = q.shape[0]
    logs, deltas = read_stats(heads, pack)
    grad = pack[:width, :].T
    for step in range(count):

        def work(step=step):
            kv = kvs[step][...]
            keys_t = kv[:, :width].T
            bias = mask_bias(scal, seqs, scal[CTX], scal[CTX] - step, size, step == 0)
            for h in range(heads):
                cut = slice(h * HD, (h + 1) * HD)
                cut_v = slice(width + h * HD, width + (h + 1) * HD)
                probs, grads = pair_back(heads, h, q[...], grad, kv, bias, logs, deltas)
                term = nn(keys_t[cut, :], grads)
                if step == 0:
                    dq_t[cut, :] = term
                    acc[:, cut] = nn(grads, q[:, cut])
                    acc[:, cut_v] = nn(probs, grad[:, cut])
                else:
                    dq_t[cut, :] += term

        if step == 0:
            work()
        else:
            pl.when(scal[CTX] >= step)(work)
    low = (dq_t[...] * (HD**-0.5)).astype(BF16)
    dq_t_out[...] = low
    dq_out[...] = low.T


def key_kernel(heads, seqs, blocks, scal, kv, acc_in, *refs):
    packs, refs = refs[: blocks - 1], refs[blocks - 1 :]
    queries, (out, acc) = refs[: blocks - 1], refs[blocks - 1 :]
    width = heads * HD
    size = kv.shape[0]
    acc[...] = acc_in[...]
    for step in range(1, blocks):

        @pl.when(scal[CTX] + step < blocks)
        def _():
            block = scal[CTX] + step
            pack = packs[step - 1]
            logs, deltas = read_stats(heads, pack)
            grad = pack[:width, :].T
            q = queries[step - 1][...]
            bias = mask_bias(scal, seqs, block, scal[CTX], size, False)
            for h in range(heads):
                cut = slice(h * HD, (h + 1) * HD)
                cut_v = slice(width + h * HD, width + (h + 1) * HD)
                probs, grads = pair_back(heads, h, q, grad, kv[...], bias, logs, deltas)
                acc[:, cut] += nn(grads, q[:, cut])
                acc[:, cut_v] += nn(probs, grad[:, cut])

    out[...] = acc[...].astype(BF16)


def split_store(scal, value, outs):
    if len(outs) == 1:
        outs[0][...] = value
        return
    mine, theirs, hold = outs
    size = mine.shape[1]
    hold[...] = value
    for slot, out in ((scal[FSDP], mine), (1 - scal[FSDP], theirs)):
        out[...] = hold[:, pl.ds(pl.multiple_of(slot * size, size), size)].astype(out.dtype)


def mlp_grads_kernel(scal, active, cotangent, two, grad, sums, *outs):
    each = len(outs) // 2
    split_store(scal, nn(active[...].T, cotangent[...]), outs[:each] + outs[2 * each :])
    split_store(scal, nn(grad[...].T, two[...]), outs[each:])
    sums[...] = jnp.zeros_like(sums)
    sums[0:1, :] = jnp.sum(grad[...].astype(F32), axis=0, keepdims=True)
    sums[1:2, :] = jnp.sum(cotangent[...].astype(F32), axis=0, keepdims=True)


def terms_kernel(count, scal, active, *refs):
    parts, (keep, send1, send2, send3, down, terms) = refs[:count], refs[count:]
    place(down, parts, scal[FSDP], 1)
    terms[...] = nn(active[...], down[...])
    size = keep.shape[0]
    for i, out in enumerate((keep, send1, send2, send3)):
        slot = jnp.bitwise_xor(scal[TP], i)
        out[...] = terms[pl.ds(pl.multiple_of(slot * size, size), size), :].astype(out.dtype)


def layer_kernel(scal, mid, vecs, tokens, keep, got1, got2, got3, out):
    size = keep.shape[0]
    out[:size, :] = tokens[...]
    total = keep[...] + got1[...].astype(F32) + got2[...].astype(F32) + got3[...].astype(F32)
    out[size:, :] = (mid[...] + total + vecs[5:6, :]).astype(BF16)


def proj_grads_kernel(scal, normed, dq_t, dkv, attn_grad, mixed_t, sums, *outs):
    value = [
        nn(dq_t[...], normed[...]),
        nn(mixed_t[...], attn_grad[...]),
        nn(dkv[...].T, normed[...]),
    ]
    split_store(scal, jnp.concatenate(value, axis=0), outs)
    width = dq_t.shape[0]
    sums[...] = jnp.zeros_like(sums)
    sums[0:1, :] = jnp.sum(attn_grad[...].astype(F32), axis=0, keepdims=True)
    column = jnp.sum(dq_t[...].astype(F32), axis=1, keepdims=True)
    sums[1:2, :width] = jnp.broadcast_to(column, (width, 128)).T[0:1, :]
    sums[2:3, :width] = jnp.sum(dkv[:, width:].astype(F32), axis=0, keepdims=True)


def small_kernel(heads, scal, sums_one, sums_mid, sums_proj, sums_mlp, shared, own):
    first = (scal[TP] == 0).astype(F32)
    width = heads * HD
    shared[...] = jnp.concatenate(
        [
            sums_one[0:2, :],
            sums_mid[0:2, :],
            sums_proj[0:1, :] * first,
            sums_mlp[1:2, :] * first,
            jnp.zeros((2, shared.shape[1]), F32),
        ],
        axis=0,
    )
    own[...] = jnp.zeros_like(own)
    own[0:1, :] = sums_mlp[0:1, :]
    own[1:3, :width] = sums_proj[1:3, :width]


def head_back_kernel(scal, full, dq, dkv, keep, send1, send2, send3, back):
    width = dq.shape[1]
    back[...] = nn(dkv[...], full[: 2 * width, :]) + nn(dq[...], full[2 * width :, :])
    size = keep.shape[0]
    for i, out in enumerate((keep, send1, send2, send3)):
        slot = jnp.bitwise_xor(scal[TP], i)
        out[...] = back[pl.ds(pl.multiple_of(slot * size, size), size), :].astype(out.dtype)


def one_back_kernel(scal, tokens, vecs, mid_grad, keep, got1, got2, got3, out, sums):
    size = keep.shape[0]
    rows = pl.ds(pl.multiple_of(scal[TP] * size, size), size)
    grad = keep[...] + got1[...].astype(F32) + got2[...].astype(F32) + got3[...].astype(F32)
    xhat, scale = standard(tokens[rows, :].astype(F32))
    total = mid_grad[...] + norm_back(xhat, scale, vecs[0:1, :], grad)
    out[...] = total.astype(BF16)
    sums[...] = jnp.zeros_like(sums)
    sums[0:1, :] = jnp.sum(grad * xhat, axis=0, keepdims=True)
    sums[1:2, :] = jnp.sum(grad, axis=0, keepdims=True)


def join_kernel(scal, part0, part1, part2, part3, tokens, layer):
    size = part0.shape[0] // 2
    for i, part in enumerate((part0, part1, part2, part3)):
        slot = jnp.bitwise_xor(scal[TP], i)
        rows = pl.ds(pl.multiple_of(slot * size, size), size)
        tokens[rows, :] = part[:size, :].astype(F32)
        layer[rows, :] = part[size:, :]


def spread_kernel(count, scal, small, *refs):
    parts, (keep, send1, send2, send3, rows) = refs[:-5], refs[-5:]
    at = 0
    for i in range(0, len(parts), count):
        value = parts[i][...]
        for part in parts[i + 1 : i + count]:
            value = value + part[...].astype(F32)
        rows[at : at + value.shape[0], :] = value
        at += value.shape[0]
    share = rows.shape[1]
    lines = small.shape[0]
    for i in range(small.shape[1] // share):
        rows[at : at + lines, :] = small[:, i * share : (i + 1) * share]
        at += lines
    if at < rows.shape[0]:
        rows[at:, :] = jnp.zeros((rows.shape[0] - at, share), F32)
    size = keep.shape[0]
    for i, out in enumerate((keep, send1, send2, send3)):
        slot = jnp.bitwise_xor(scal[CTX], i)
        out[...] = rows[pl.ds(pl.multiple_of(slot * size, 16), size), :].astype(out.dtype)


def collect_kernel(owners, scal, part0, part1, part2, part3, *refs):
    (query, out, key, value), vectors, heads, rows = refs[:4], refs[4:10], refs[10:13], refs[13]
    size = part0.shape[0]
    for i, part in enumerate((part0, part1, part2, part3)):
        slot = jnp.bitwise_xor(scal[CTX], i)
        rows[pl.ds(pl.multiple_of(slot * size, 16), size), :] = part[...].astype(F32)
    at = 0
    for result in (query, out, key, value):
        result[...] = rows[at : at + result.shape[0], :]
        at += result.shape[0]
    own = rows[pl.ds(pl.multiple_of(at + scal[FSDP] * 16, 16), 16), :]
    for i, vector in enumerate(vectors):
        vector[...] = own[i]
    lines = [rows[at + 16 * i + 8 : at + 16 * i + 16, :] for i in range(owners)]
    lines = jnp.concatenate(lines, axis=1)
    for i, result in enumerate(heads):
        count, each = result.shape
        for h in range(count):
            line = jnp.zeros((1, each), F32)
            for owner in range(owners):
                first = (h * owners + owner) * each
                found = lines[i : i + 1, first : first + each]
                line = jnp.where(scal[FSDP] == owner, found, line)
            result[h : h + 1, :] = line


def swap_fsdp(value):
    return lax.ppermute(value, "fsdp", [(0, 1), (1, 0)])


def swap_tp(value, bits):
    return lax.ppermute(value, "tp", [(i, i ^ bits) for i in range(4)])


def gather_tp(value):
    far = swap_tp(value, 2)
    near = swap_tp(value, 1)
    return value, near, far, swap_tp(far, 1)


def down_ctx(value, step):
    count = lax.axis_size("ctx")
    return lax.ppermute(value, "ctx", [(i + step, i) for i in range(count - step)])


def chain_one(value):
    part = value.astype(BF16)
    return part, lax.ppermute(part, "ctx", [(0, 1), (3, 2)])


def chain_two(part, got):
    part = (part.astype(F32) + got.astype(F32)).astype(BF16)
    return part, lax.ppermute(part, "ctx", [(1, 2), (2, 1)])


def chain_three(part, got):
    part = (part.astype(F32) + got.astype(F32)).astype(BF16)
    return part, lax.ppermute(part, "ctx", [(1, 0), (2, 3)])


def sum_small(shared, own, owners, other):
    for bits in (1, 2):
        shared = shared + swap_tp(shared, bits)
    both = after(jnp.concatenate([shared, own], axis=0), other)
    if owners == 2:
        return both + swap_fsdp(both)
    return lax.psum(both, "fsdp")


def swap_ctx(value, bits):
    return lax.ppermute(value, "ctx", [(i, i ^ bits) for i in range(4)])


def shards(
    tokens,
    g_attn,
    s_attn,
    w_query,
    b_query,
    w_key,
    w_value,
    b_value,
    w_out,
    b_out,
    g_mlp,
    s_mlp,
    w_up,
    b_up,
    w_down,
    b_down,
    cotangent,
    lengths,
):
    owners = lax.axis_size("fsdp")
    blocks = lax.axis_size("ctx")
    pair = owners == 2
    count = 2 if pair else 1
    size, model = tokens.shape
    heads = b_query.shape[0]
    width = heads * HD
    hidden = w_up.shape[1]
    seqs = lengths.shape[1]
    quarter = size // 4
    ctx = lax.axis_index("ctx")
    fsdp = lax.axis_index("fsdp")
    tp = lax.axis_index("tp")
    scal = jnp.concatenate([jnp.stack([ctx, fsdp, tp]).astype(jnp.int32), lengths[0]])

    def fetch(value, axis):
        if pair:
            return (value, swap_fsdp(value))
        return (lax.all_gather(value, "fsdp", axis=axis, tiled=True),)

    share = model // owners
    inner = (ctx == 1) | (ctx == 2)
    lanes = max(share, hidden // owners)
    vectors = (g_attn, s_attn, b_out, g_mlp, s_mlp, b_down, b_up, b_query, b_value)
    anywhere = pl.BlockSpec(memory_space=pl.ANY)
    pack = pl.pallas_call(
        functools.partial(pack_kernel, heads),
        out_shape=shape((4 * width + 16, lanes), BF16),
        in_specs=[pl.BlockSpec(memory_space=pltpu.SMEM)] + [anywhere] * 13,
        out_specs=pl.BlockSpec(memory_space=pltpu.VMEM),
        scratch_shapes=[pltpu.VMEM(vector.shape, BF16) for vector in vectors]
        + [pltpu.SemaphoreType.DMA((13,))],
        name="pack",
    )(scal, w_key.T, w_value.T, w_query.T, w_out, *vectors)
    if pair:
        packs = (pack, swap_fsdp(pack))
    else:
        every = lax.all_gather(pack, "fsdp", axis=0)
        packs = tuple(every[i] for i in range(owners))
    half = lax.dynamic_slice_in_dim(tokens, (tp % 2) * (size // 2), size // 2, 0)
    tokens_near = lax.all_gather(half, "ctx", axis=0, tiled=True)
    up_parts = fetch(after(w_up, packs[-1]), 0)
    down_parts = fetch(after(w_down, up_parts[-1]), 1)

    state_shape = shape((8, size), F32)
    acc_shape = shape((width, size), F32)
    full, out_full, vecs, normed, q, kv, state, acc = call(
        functools.partial(first_kernel, heads, seqs, len(packs)),
        [
            shape((3 * width, model), BF16),
            shape((width, model), BF16),
            shape((16, model), F32),
            shape((size, model), BF16),
            shape((size, width), BF16),
            shape((size, 2 * width), BF16),
            state_shape,
            acc_shape,
        ],
        scal,
        tokens,
        *packs,
        cost=3.5,
        name="attend_first",
    )
    tokens_far = swap_tp(after(tokens_near, state, up_parts[-1]), 1)
    out_all = lax.all_gather(after(out_full, tokens_near), "tp", axis=0, tiled=True)
    *rest, mixed_t, mix_t, logs = call(
        functools.partial(others_kernel, heads, seqs, blocks),
        [shape((size, 2 * width), BF16)] * (blocks - 1)
        + [shape((size, width), BF16)] * (blocks - 1)
        + [shape((width, size), BF16), acc_shape, state_shape],
        scal,
        vecs,
        full,
        q,
        state,
        acc,
        tokens_near,
        tokens_far,
        scratch=[
            pltpu.VMEM((8, size), F32),
            pltpu.VMEM((width, size), F32),
            pltpu.VMEM((size, model), BF16),
        ],
        cost=7.0,
        name="attend_others",
    )
    kvs, upper_q = [kv] + rest[: blocks - 1], rest[blocks - 1 :]

    mixed_parts = gather_tp(mixed_t)
    row_quarter = shape((quarter, model), BF16)
    sent = [shape((quarter, model), F32), row_quarter, row_quarter, row_quarter]
    wide = shape((size, hidden), BF16)
    mid_quarter, cot_quarter, two, active, grad_upper, *back = call(
        functools.partial(mlp_kernel, count),
        [
            shape((quarter, model), F32),
            row_quarter,
            shape((size, model), BF16),
            wide,
            wide,
        ]
        + sent,
        scal,
        tokens,
        cotangent,
        vecs,
        *mixed_parts,
        out_all,
        *up_parts,
        *down_parts,
        scratch=[
            pltpu.VMEM((model, hidden), BF16),
            pltpu.VMEM((hidden, model), BF16),
            pltpu.VMEM((size, model), F32),
            pltpu.VMEM((4 * width, size), BF16),
        ],
        cost=7,
        name="mlp",
    )
    got_mid = [swap_tp(back[i], i) for i in range(1, 4)]

    def grad_outs(lines, held):
        if pair:
            part = (lines, share)
            return [shape(part, F32), shape(part, BF16)], [pltpu.VMEM((held, model), F32)]
        return [shape((lines, model), F32)], []

    def owned(parts):
        if pair:
            return parts[0], swap_fsdp(parts[1])
        return (lax.psum_scatter(parts[0], "fsdp", scatter_dimension=1, tiled=True),)

    def summed(parts):
        return parts[0] + parts[1].astype(F32) if len(parts) == 2 else parts[0]

    sums_shape = shape((8, model), F32)
    outs, scratch = grad_outs(hidden, hidden)
    sums_mlp, *parts = call(
        mlp_grads_kernel,
        [sums_shape] + outs + outs,
        scal,
        after(active, got_mid[0]),
        cotangent,
        two,
        grad_upper,
        scratch=scratch,
        cost=3.2,
        name="mlp_grads",
    )
    own_up = owned(parts[count:])
    mid_grad, attn_quarter, sums_mid = call(
        mid_back_kernel,
        [shape((quarter, model), F32), row_quarter, sums_shape],
        scal,
        mid_quarter,
        cot_quarter,
        after(vecs, sums_mlp),
        back[0],
        *got_mid,
        cost=1.0,
        name="mid_back",
    )
    attn_parts = gather_tp(attn_quarter)
    own_down = owned([after(part, own_up[-1]) for part in parts[:count]])
    one_up = chain_one(summed(own_up))
    attn_grad, pack = call(
        functools.partial(out_back_kernel, heads),
        [shape((size, model), BF16), shape((width + 32, size), BF16)],
        scal,
        after(out_full, own_up[-1]),
        mix_t,
        logs,
        *attn_parts,
        cost=1.1,
        name="out_back",
    )
    upper = [down_ctx(pack, step) for step in range(1, blocks)]
    dq, dq_t, dkv = call(
        functools.partial(query_kernel, heads, seqs, blocks),
        [shape((size, width), BF16), shape((width, size), BF16), shape((size, 2 * width), F32)],
        scal,
        q,
        pack,
        *kvs,
        scratch=[pltpu.VMEM((width, size), F32)],
        cost=5.2,
        name="query_back",
    )
    (dkv,) = call(
        functools.partial(key_kernel, heads, seqs, blocks),
        [shape((size, 2 * width), BF16)],
        scal,
        kv,
        dkv,
        *upper,
        *upper_q,
        scratch=[pltpu.VMEM((size, 2 * width), F32)],
        cost=7.0,
        name="key_back",
    )
    two_up = chain_two(*one_up)
    one_down = chain_one(summed(own_down))
    back = call(
        head_back_kernel,
        sent,
        scal,
        full,
        dq,
        after(dkv, one_up[1]),
        scratch=[pltpu.VMEM((size, model), F32)],
        cost=1.5,
        name="head_back",
    )
    got_one = [swap_tp(back[i], i) for i in range(1, 4)]
    outs, scratch = grad_outs(4 * width, 4 * width)
    sums_proj, *parts = call(
        proj_grads_kernel,
        [sums_shape] + outs,
        scal,
        after(normed, got_one[0]),
        dq_t,
        dkv,
        attn_grad,
        mixed_t,
        scratch=scratch,
        cost=2.5,
        name="proj_grads",
    )
    own_proj = owned(parts)
    terms = call(
        functools.partial(terms_kernel, count),
        sent,
        scal,
        after(active, sums_proj),
        *down_parts,
        scratch=[pltpu.VMEM((hidden, model), BF16), pltpu.VMEM((size, model), F32)],
        cost=1.5,
        name="terms",
    )
    got_terms = [swap_tp(terms[i], i) for i in range(1, 4)]
    token_quarter, sums_one = call(
        one_back_kernel,
        [row_quarter, sums_shape],
        scal,
        tokens,
        vecs,
        after(mid_grad, terms[0]),
        back[0],
        *got_one,
        cost=1.0,
        name="one_back",
    )
    small = call(
        functools.partial(small_kernel, heads),
        [sums_shape, sums_shape],
        scal,
        after(sums_one, two_up[1], one_down[1]),
        sums_mid,
        sums_proj,
        sums_mlp,
        cost=0.6,
        name="small",
    )
    (both,) = call(
        layer_kernel,
        [shape((2 * quarter, model), BF16)],
        scal,
        mid_quarter,
        vecs,
        token_quarter,
        terms[0],
        *got_terms,
        name="layer",
    )
    token_parts = gather_tp(both)
    three_up = chain_three(*two_up)
    two_down = chain_two(*one_down)
    three_down = chain_three(*two_down)
    small = sum_small(*small, owners, own_proj[-1])
    lines = -(-(4 * width + 16 * owners) // 64) * 64
    piece = shape((lines // 4, share), BF16)
    pieces = call(
        functools.partial(spread_kernel, count),
        [shape((lines // 4, share), F32), piece, piece, piece],
        scal,
        after(small, two_up[1], one_down[1]),
        *own_proj,
        scratch=[pltpu.VMEM((lines, share), F32)],
        name="spread",
    )
    got = [swap_ctx(pieces[i], i) for i in range(1, 4)]
    piece = (pieces[0] + sum(part.astype(F32) for part in got)).astype(BF16)
    piece = after(piece, three_up[1], two_down[1])
    each = shape((width, share), F32)
    vector = shape((share,), F32)
    dw_query, dw_out, dw_key, dw_value, *smalls = call(
        functools.partial(collect_kernel, owners),
        [each] * 4
        + [vector] * 6
        + [shape(bias.shape, F32) for bias in (b_up, b_query, b_value)],
        scal,
        piece,
        *[swap_ctx(piece, i) for i in range(1, 4)],
        scratch=[pltpu.VMEM((lines, share), F32)],
        name="collect",
    )
    d_tokens, layer_out = call(
        join_kernel,
        [shape((size, model), F32), shape((size, model), BF16)],
        scal,
        *token_parts,
        cost=2.0,
        name="join",
    )

    dw_down = jnp.where(inner, *three_down).astype(F32)
    dw_up = jnp.where(inner, *three_up).astype(F32).T
    dg_attn, ds_attn, dg_mlp, ds_mlp, db_out, db_down, db_up, db_query, db_value = smalls
    return (
        layer_out,
        d_tokens,
        dg_attn,
        ds_attn,
        dw_query.T,
        db_query,
        dw_key.T,
        dw_value.T,
        db_value,
        dw_out,
        db_out,
        dg_mlp,
        ds_mlp,
        dw_up,
        db_up,
        dw_down,
        db_down,
    )


def solution(mesh):
    return jax.shard_map(
        shards,
        mesh=mesh,
        in_specs=(
            P(("fsdp", "ctx"), None),
            P("fsdp"),
            P("fsdp"),
            P("fsdp", "tp"),
            P("tp", "fsdp"),
            P("fsdp", "tp"),
            P("fsdp", "tp"),
            P("tp", "fsdp"),
            P("tp", "fsdp"),
            P("fsdp"),
            P("fsdp"),
            P("fsdp"),
            P("fsdp", "tp"),
            P("tp", "fsdp"),
            P("tp", "fsdp"),
            P("fsdp"),
            P(("fsdp", "ctx"), None),
            P("fsdp", None),
        ),
        out_specs=(
            P(("fsdp", "ctx"), None),
            P(("fsdp", "ctx"), None),
            P("fsdp"),
            P("fsdp"),
            P("fsdp", "tp"),
            P("tp", "fsdp"),
            P("fsdp", "tp"),
            P("fsdp", "tp"),
            P("tp", "fsdp"),
            P("tp", "fsdp"),
            P("fsdp"),
            P("fsdp"),
            P("fsdp"),
            P("fsdp", "tp"),
            P("tp", "fsdp"),
            P("tp", "fsdp"),
            P("fsdp"),
        ),
        check_vma=False,
    )
```
